512 devices in a mesh: horiz: 128 (over z, y, core), lev: 4 (over x).
Axes of the slice: x: 4, y: 8, z: 8, core: 2. Of those that a mesh axis runs over, the one named last changes fastest.
Arguments:
- jacobian: bfloat16 [8192, 2, 136, 200], P('horiz', None, 'lev'), may hold values from -0.375 to 0.375
- obs_tile: int32 [8192, 1], P('horiz'), may hold values from 0 to 127; in each aligned block of 64 rows (0 to 63, 64 to 127, ...) at most 2 rows name the same one
- obs_column: int32 [8192], P('horiz'), may hold values from 0 to 511
- obs_weight: float32 [8192], P('horiz'), may hold values from 0.25 to 4
- innovation: float32 [8192, 200], P('horiz'), may hold values from -12 to 12
- precision_off: float32 [200, 200], replicated, may hold values from -0.03 to 0.03
- vertical_factor: float32 [2, 136, 136], replicated, may hold values from -0.05 to 0.05
Outputs:
- increment: float32 [136, 2, 65536], P('lev', None, 'horiz')
- residual: float32 [136, 2, 65536], P('lev', None, 'horiz')
The draws below stay inside these ranges and needn't reach their ends.
Inputs may be any that keep to these rules, and one draw needn't show every extreme that they name: `obs_tile`: among the 64 observations of one index of horiz, at most 2 fall in one tile, and some tile takes exactly 2.
All inputs are finite; a program needn't handle non-finite values.
Results may differ from the reference program's by a relative error of at most 0.008.
Values may be sent and summed in bfloat16 or wider, within the bound.
A program may use at most 128 MiB of HBM per device.

```python
import math
import jax
import jax.numpy as jnp
import numpy as np
from jax import lax

CH = 200
LEV = 136
COLS = 512
OBS_DEV = 64
ITERS = 2
CAP = 2
OBS = 8192
N_HORIZ = 128


def draw_innovation(key, part):
    key = jax.random.fold_in(key, 7)
    positions = jnp.arange(OBS, dtype=jnp.float32)
    scales = 1.0 + 2.0 * positions / max(OBS - 1, 1)
    values = jnp.clip(jax.random.normal(key, (OBS, CH), jnp.float32), -4.0, 4.0)
    return values * scales[:, None]


def plant(values, rng, least, high):
    extent = values.shape
    spot = [jax.random.randint(jax.random.fold_in(rng, axis), (), 0, extent[axis]) for axis in range(len(extent))]
    values = values.at[tuple(spot)].set(least)
    longest = extent.index(max(extent))
    spot[longest] = (spot[longest] + 1) % extent[longest]
    return values.at[tuple(spot)].set(high)


def block_scale(rng, dims, split, smallest, largest):
    loudness, own = 1.0, jax.random.fold_in(rng, 6)
    for axis_at, parts in split:
        steps = jnp.exp(jax.random.uniform(jax.random.fold_in(own, axis_at), (parts,), jnp.float32, smallest / len(split), largest / len(split)))
        loudness = loudness * jnp.repeat(steps, dims[axis_at] // parts).reshape([-1 if axis == axis_at else 1 for axis in range(len(dims))])
    return loudness


def deal_out(rng, own, number, rows, amount, top, bound, lean):
    sequence = jax.random.permutation(rng, amount)
    packed, ordinary = load_shares(amount, rows * top, bound, lean, True), load_shares(amount, rows * top, bound, lean, False)
    places = jnp.arange(amount)

    def named(tallies, offset_by):
        used = int((tallies > 0).sum())
        fixed = max(1, used // 4)
        shifted = fixed + (places - fixed + offset_by * (used - fixed)) % max(1, amount - fixed)
        return jnp.zeros((amount,), jnp.int32).at[sequence[jnp.where(places < fixed, places, shifted)]].set(jnp.asarray(tallies, jnp.int32))

    tallies = jnp.where(number % 4 == 0, named(packed, number // 4), named(ordinary, number - number // 4 - 1))
    mixed = jax.random.permutation(jax.random.fold_in(own, 3), amount)
    donor, receiver = mixed[0:amount // 2 * 2:2], mixed[1:amount // 2 * 2:2]
    slack = jnp.minimum(tallies[donor] - 1, bound - tallies[receiver]) // 2
    slack = jnp.where((donor == sequence[0]) | (receiver == sequence[0]) | (tallies[receiver] == 0), 0, jnp.maximum(slack, 0))
    shifted = jax.random.randint(jax.random.fold_in(own, 4), (amount // 2,), 0, 1 << 20) % (slack + 1)
    tallies = tallies.at[donor].add(-shifted).at[receiver].add(shifted)
    labels = jnp.searchsorted(jnp.cumsum(tallies), jnp.arange(rows * top), side="right").astype(jnp.int32)
    grid = labels.reshape(top, rows).T
    grid = grid[jax.random.permutation(jax.random.fold_in(own, 1), rows)]
    offset_by = jax.random.randint(jax.random.fold_in(own, 2), (rows, 1), 0, top)
    return jnp.take_along_axis(grid, (jnp.arange(top)[None, :] + offset_by) % top, axis=1)


def load_shares(number_of, total, limit, lean, full):
    loads = [(1 << 20) // math.isqrt(standing ** lean) + 1 for standing in range(1, number_of + 1)]
    largest = limit if full else min(limit, max(-(-total // number_of), total * loads[0] // sum(loads)))
    least = 1 if total - largest >= number_of - 1 else 0
    holding, rest = [largest] + [least] * (number_of - 1), total - largest - least * (number_of - 1)
    while rest > 0:
        free = [i for i in range(1, number_of) if holding[i] < largest] or [i for i in range(1, number_of) if holding[i] < limit]
        whole, left = sum([loads[i] for i in free]), rest
        for i in free:
            more = min(limit - holding[i], max(1, left * loads[i] // whole), rest)
            holding[i] = holding[i] + more
            rest = rest - more
    return np.array(holding)


def gaussian(key, shape, spread, limit, pieces=(), kind=jnp.bfloat16):
    gain = block_scale(key, shape, pieces, -0.22, 0.18) if pieces else 1.0
    result = jax.random.normal(key, shape, jnp.float32) * spread * gain
    return jnp.minimum(jnp.maximum(result, -limit), limit).astype(kind)


def setup_inputs(seed: int = 0) -> dict:
    key_of = jax.random.split(jax.random.key(seed), 8)
    jacobian = gaussian(key_of[0], (OBS, 2, LEV, CH), (2 * LEV) ** -0.5, 0.375, ((0, 128), (2, 4)))
    obs_tile_keys = jax.random.split(jax.random.fold_in(key_of[1], 1), OBS // OBS_DEV)
    obs_tile_turns = jax.random.permutation(jax.random.fold_in(key_of[1], 3), OBS // OBS_DEV)
    obs_tile = jax.vmap(lambda own, number: deal_out(jax.random.fold_in(key_of[1], 2), own, number, OBS_DEV, N_HORIZ, 1, CAP, 2))(obs_tile_keys, obs_tile_turns).reshape((OBS, 1))
    obs_column = plant(jax.random.randint(key_of[2], (OBS,), 0, COLS), jax.random.fold_in(key_of[2], 1), 0, COLS - 1).astype(jnp.int32)
    obs_weight = jnp.clip(jnp.exp(math.log(4.0) - 2.7725887 * jax.random.uniform(key_of[3], (OBS,), jnp.float32) ** block_scale(key_of[3], (OBS,), ((0, 128),), -0.2, 0.2)), 0.25, 4.0)
    innovation = draw_innovation(jax.random.fold_in(key_of[7], 71), 0)
    precision_off = jnp.clip(jax.random.uniform(key_of[5], (CH, CH), jnp.float32, -0.03, 0.03), -0.03, 0.03)
    vertical_factor = jnp.clip(jax.random.uniform(key_of[6], (2, LEV, LEV), jnp.float32, -0.05, 0.05), -0.05, 0.05)
    return dict(jacobian=jacobian, obs_tile=obs_tile, obs_column=obs_column, obs_weight=obs_weight, innovation=innovation, precision_off=precision_off, vertical_factor=vertical_factor)


def reference(jacobian, obs_tile, obs_column, obs_weight, innovation, precision_off, vertical_factor):
    highest = lax.Precision.HIGHEST
    obs_total = jacobian.shape[0]
    levels = jacobian.shape[2]
    channels = jacobian.shape[3]
    column_total = COLS * N_HORIZ
    factor = jnp.eye(levels, dtype=jnp.float32)[None] + vertical_factor
    precision_matrix = jnp.eye(channels, dtype=jnp.float32) + 0.5 * (precision_off + precision_off.T)
    location = (obs_tile[:, 0] * COLS + obs_column).astype(jnp.int32)
    block_count = obs_total // OBS_DEV
    jac_blocks = jacobian.reshape(block_count, OBS_DEV, 2, levels, channels)
    where_blocks = location.reshape(block_count, OBS_DEV)

    def forward(state):
        return jnp.einsum("vij,jvc->ivc", factor, state, precision=highest)

    def backward(state):
        return jnp.einsum("vij,ivc->jvc", factor, state, precision=highest)

    def images(state):
        def single(inputs):
            jac_part, where_part = inputs
            columns = jnp.take(state, where_part, axis=2).astype(jnp.bfloat16).astype(jnp.float32)
            return jnp.einsum("ovic,ivo->oc", jac_part.astype(jnp.float32), columns)
        return lax.map(single, (jac_blocks, where_blocks)).reshape(obs_total, channels)

    def weigh(values):
        return (obs_weight[:, None] * jnp.dot(values, precision_matrix, precision=highest)).astype(jnp.bfloat16)

    def adjoint(weighted):
        weight_blocks = weighted.reshape(block_count, OBS_DEV, channels)

        def single(inputs):
            jac_part, weight_part = inputs
            return jnp.einsum("ovic,oc->oiv", jac_part.astype(jnp.float32), weight_part.astype(jnp.float32))
        terms = lax.map(single, (jac_blocks, weight_blocks)).reshape(obs_total, levels, 2)
        summed = jax.ops.segment_sum(terms, location, num_segments=column_total)
        return jnp.transpose(summed, (1, 2, 0))

    def normal(direction):
        return direction + backward(adjoint(weigh(images(forward(direction)))))

    rhs = backward(adjoint(weigh(innovation)))
    increment = jnp.zeros_like(rhs)
    residual = rhs
    direction = rhs
    norm_now = jnp.sum(residual * residual)
    for iteration in range(ITERS):
        image = normal(direction)
        step_length = norm_now / jnp.sum(direction * image)
        increment = increment + step_length * direction
        residual = residual - step_length * image
        norm_next = jnp.sum(residual * residual)
        direction = residual + (norm_next / norm_now) * direction
        norm_now = norm_next
    return increment, residual
```

```python
import functools

import jax
import jax.numpy as jnp
from jax import lax
from jax.experimental import pallas as pl
from jax.experimental.pallas import tpu as pltpu
from jax.sharding import PartitionSpec as P

MESH = pl.DeviceIdType.MESH
HIGHEST = lax.Precision.HIGHEST
COLS = 512
SLAB = 64
ROWS = 40
GROUP = 8
COL_LANE = 63
SUM_LANE = 40


def nt(a, b, precision=None):
    return lax.dot_general(
        a, b, (((1,), (1,)), ((), ())), precision=precision, preferred_element_type=jnp.float32
    )


def nn(a, b, precision=None):
    return lax.dot_general(
        a, b, (((1,), (0,)), ((), ())), precision=precision, preferred_element_type=jnp.float32
    )


def split(x):
    high = x.astype(jnp.bfloat16)
    return high, (x - high.astype(jnp.float32)).astype(jnp.bfloat16)


def iota(shape, dim):
    return lax.broadcasted_iota(jnp.int32, shape, dim)


def kernel(
    tiles,
    bands,
    jac,
    meta,
    innovation,
    precision_off,
    vertical,
    increment,
    residual,
    jpad,
    rmat,
    coef,
    picks,
    sends,
    equal,
    tbuf,
    ibuf,
    sbuf,
    rbuf,
    w0_buf,
    im0_buf,
    w1_buf,
    im1_buf,
    t_send,
    t_recv,
    i_send,
    i_recv,
    s_send,
    s_recv,
):
    me = lax.axis_index("horiz")
    lev = lax.axis_index("lev")
    obs = innovation.shape[0]
    channels = innovation.shape[1]
    slabs, band, _ = jac.shape
    levels = vertical.shape[1]
    f32, bf16 = jnp.float32, jnp.bfloat16

    barrier = pltpu.get_barrier_semaphore()

    @pl.loop(1, tiles)
    def _(k):
        peer = lax.rem(me + k, tiles)
        pl.semaphore_signal(barrier, inc=1, device_id={"horiz": peer}, device_id_type=MESH)

    for k in range(1, bands):
        peer = lax.rem(lev + k, bands)
        pl.semaphore_signal(barrier, inc=1, device_id={"lev": peer}, device_id_type=MESH)

    @pl.loop(0, slabs, unroll=8)
    def _(s):
        start = pl.multiple_of(s * SLAB, SLAB)
        jpad[pl.ds(start + 32, 32), :] = jnp.zeros((32, channels), bf16)
        jpad[pl.ds(start, band), :] = jac[s]

    tile_of = meta[:, 0:1]
    column_of = meta[:, 1:2]
    weight = meta[:, 2:3]
    onehot = (tile_of == iota((obs, tiles), 1).astype(f32)).astype(f32)
    same = nt(onehot.astype(bf16), onehot.astype(bf16))
    earlier = iota((obs, obs), 1) < iota((obs, obs), 0)
    position = jnp.sum(jnp.where(earlier, same, 0.0), axis=1, keepdims=True)
    first = jnp.where(position < 0.5, onehot, 0.0)
    second = jnp.where(position > 0.5, onehot, 0.0)
    picks[:, 0:tiles] = first.astype(bf16)
    picks[:, tiles : 2 * tiles] = second.astype(bf16)
    sends[0:tiles, :] = jnp.concatenate([first, first], axis=0).T.astype(bf16)
    sends[tiles : 2 * tiles, :] = jnp.concatenate([second, second], axis=0).T.astype(bf16)

    off = precision_off[...]
    eye_c = (iota((channels, channels), 0) == iota((channels, channels), 1)).astype(f32)
    rmat[...] = eye_c + 0.5 * (off + off.T)
    row = iota((SLAB, levels), 0)
    own = ((iota((SLAB, levels), 1) == lev * band + row) & (row < band)).astype(f32)
    spread_row = iota((levels, bands * ROWS), 0)
    spread_lane = iota((levels, bands * ROWS), 1)
    spread = jnp.zeros((levels, bands * ROWS), f32)
    for m in range(bands):
        level = spread_lane - m * ROWS
        spread += (
            (level >= 0) & (level < band) & (spread_row == m * band + level)
        ).astype(f32)
    eye_l = (iota((levels, levels), 0) == iota((levels, levels), 1)).astype(f32)
    for v in range(2):
        factor = eye_l + vertical[v]
        both = nt(nn(own, factor, HIGHEST), factor, HIGHEST)
        back = nt(own, factor, HIGHEST)
        coef[v * SLAB : (v + 1) * SLAB, :] = nn(both, spread, HIGHEST)
        coef[(2 + v) * SLAB : (3 + v) * SLAB, :] = nn(back, spread, HIGHEST)

    def weigh(values):
        return weight * nn(values, rmat[...], HIGHEST)

    def adjoint(use, high, low):
        both = jnp.concatenate([high, low], axis=0)
        lane = lax.rem(iota((ROWS, 2 * obs), 1), obs)

        def step(g, sums):
            start = pl.multiple_of(g * (2 * GROUP * SLAB), 2 * GROUP * SLAB)
            product = nt(jpad[pl.ds(start, 2 * GROUP * SLAB), :], both)
            sums = list(sums)
            for j in range(GROUP):
                mine = lane == g * GROUP + j
                for v in range(2):
                    at = (2 * j + v) * SLAB
                    sums[v] = sums[v] + jnp.where(mine, product[at : at + ROWS, :], 0.0)
            return tuple(sums)

        zero = jnp.zeros((ROWS, 2 * obs), f32)
        t0, t1 = lax.fori_loop(0, obs // GROUP, step, (zero, zero))
        t0 = t0 + pltpu.roll(t0, obs, 1)
        t1 = t1 + pltpu.roll(t1, obs, 1)
        tbuf[use, lev] = jnp.where(iota((ROWS, 2 * obs), 1) < obs, t0, t1)

    def between_bands(buf, use, send_sem, recv_sem):
        copies = []
        for k in range(1, bands):
            copy = pltpu.make_async_remote_copy(
                src_ref=buf.at[use, lev],
                dst_ref=buf.at[use, lev],
                send_sem=send_sem.at[use, k],
                recv_sem=recv_sem.at[use, k],
                device_id={"lev": lax.rem(lev + k, bands)},
                device_id_type=MESH,
            )
            copy.start()
            copies.append(copy)
        for copy in copies:
            copy.wait()

    def columns(use):
        gathered = tbuf[use].reshape(bands * ROWS, 2 * obs)
        mapped = nn(coef[...], gathered, HIGHEST)
        diagonal = iota((2 * SLAB, 2 * obs), 0) // SLAB == iota((2 * SLAB, 2 * obs), 1) // obs
        out = []
        for part in range(2):
            block = jnp.where(diagonal, mapped[part * 2 * SLAB : (part + 1) * 2 * SLAB, :], 0.0)
            high, low = split(block)
            slots = nt(sends[...], jnp.concatenate([high, low], axis=0))
            out.append(slots[:, 0 : 2 * SLAB] + slots[:, 2 * SLAB :])
        return out

    def exchange(use):
        @pl.loop(1, tiles)
        def _(k):
            peer = lax.rem(me + k, tiles)
            pltpu.make_async_remote_copy(
                src_ref=sbuf.at[use, peer],
                dst_ref=rbuf.at[use, me],
                send_sem=s_send.at[use],
                recv_sem=s_recv.at[use],
                device_id={"horiz": peer},
                device_id_type=MESH,
            ).start()

        rbuf[use, me] = sbuf[use, me]

    def arrived(use):
        part = rbuf.at[use, pl.ds(0, tiles - 1)]
        pltpu.make_async_copy(part, part, s_recv.at[use]).wait()

    def left(use):
        part = sbuf.at[use, pl.ds(0, tiles - 1)]
        pltpu.make_async_copy(part, part, s_send.at[use]).wait()

    def put(use, slots):
        sbuf[use, :, 0, :] = slots[0:tiles, :]
        sbuf[use, :, 1, :] = slots[tiles : 2 * tiles, :]

    def got(use):
        return jnp.concatenate([rbuf[use, :, 0, :], rbuf[use, :, 1, :]], axis=0)

    def sum_at_tiles(use, first_time):
        slots = got(use)
        if first_time:
            ids = [slots[s * tiles : (s + 1) * tiles, COL_LANE : COL_LANE + 1] for s in range(2)]
            wide = [jnp.broadcast_to(one, (tiles, tiles)) for one in ids]
            tall = [one.T for one in wide]
            for a in range(2):
                for b in range(2):
                    equal[a * tiles : (a + 1) * tiles, b * tiles : (b + 1) * tiles] = jnp.where(
                        (wide[a] == tall[b]) & (wide[a] > 0.5), 1.0, 0.0
                    ).astype(bf16)
        high, low = split(slots)
        sums = nn(equal[...], jnp.concatenate([high, low], axis=1))
        put(use + 1, sums[:, 0 : 2 * SLAB] + sums[:, 2 * SLAB :])
        return slots

    def images(use, from_use):
        high, low = split(got(from_use))
        chosen = nn(picks[...], jnp.concatenate([high, low], axis=1))
        group_row = lax.rem(iota((2 * GROUP, 2 * SLAB), 0), GROUP)
        for g in range(obs // GROUP):
            rows = chosen[g * GROUP : (g + 1) * GROUP, :]
            pair = jnp.concatenate([rows[:, 0 : 2 * SLAB], rows[:, 2 * SLAB :]], axis=0)
            lhs = jnp.concatenate(
                [jnp.where(group_row == j, pair, 0.0) for j in range(GROUP)], axis=1
            ).astype(bf16)
            start = g * 2 * GROUP * SLAB
            part = nn(lhs, jpad[start : start + 2 * GROUP * SLAB, :])
            ibuf[use, lev, g * GROUP : (g + 1) * GROUP, :] = part[0:GROUP, :] + part[GROUP:, :]
        between_bands(ibuf, use, i_send, i_recv)
        total = ibuf[use, 0]
        for m in range(1, bands):
            total = total + ibuf[use, m]
        return total

    w0 = weigh(innovation[...]).astype(bf16)
    w0_buf[...] = w0.astype(f32)
    adjoint(0, w0, jnp.zeros_like(w0))
    pl.semaphore_wait(barrier, tiles - 1 + bands - 1)
    between_bands(tbuf, 0, t_send, t_recv)
    c0, u0 = columns(0)
    column_rhs = jnp.where(
        (iota((2 * obs, 2 * SLAB), 1) == COL_LANE) & (iota((2 * obs, 2 * SLAB), 0) < obs),
        jnp.concatenate([column_of, column_of], axis=0) + 1.0,
        0.0,
    )
    high, low = split(column_rhs)
    put(0, c0 + nn(sends[...], high) + nn(sends[...], low))
    exchange(0)
    put(4, u0)
    arrived(0)
    first_slots = sum_at_tiles(0, True)
    exchange(1)
    exchange(4)
    slot_column = first_slots[:, COL_LANE : COL_LANE + 1]
    arrived(1)
    im0 = images(0, 1)
    im0_buf[...] = im0
    w1 = weigh(im0)
    w1_buf[...] = w1
    adjoint(1, *split(w1))
    between_bands(tbuf, 1, t_send, t_recv)
    c1, u1 = columns(1)
    put(2, c1)
    exchange(2)
    put(5, u1)
    arrived(2)
    sum_at_tiles(2, False)
    exchange(3)
    exchange(5)
    arrived(3)
    im1 = images(1, 3)
    w2 = weigh(im1)
    adjoint(2, *split(w2))
    between_bands(tbuf, 2, t_send, t_recv)
    _, u2 = columns(2)

    w0, im0, w1 = w0_buf[...], im0_buf[...], w1_buf[...]
    lane = iota((1, 2 * SLAB), 1)
    scalars = jnp.zeros((1, 2 * SLAB), f32)
    for at, (a, b) in enumerate(((w0, im0), (w1, im0), (w1, im1), (w2, im0), (w2, im1))):
        one = jnp.sum(jnp.sum(a * b, axis=1, keepdims=True), axis=0, keepdims=True)
        scalars = scalars + jnp.where(lane == SUM_LANE + at, one, 0.0)
    put(6, u2 + scalars)
    exchange(6)
    arrived(4)
    arrived(5)
    arrived(6)
    u2 = got(6)
    sums = jnp.sum(u2[0:tiles, :], axis=0, keepdims=True)
    g00, g01, g11, g02, g12 = (
        jnp.sum(jnp.where(lane == SUM_LANE + at, sums, 0.0), axis=1, keepdims=True)
        for at in range(5)
    )
    a0 = g00 / (g00 + g01)
    keep = 1.0 - a0
    rr1 = keep * keep * g00 - 2.0 * a0 * keep * g01 + a0 * a0 * g11
    k0 = keep + rr1 / g00
    k1 = -a0
    mixed = k0 + k1
    curvature = k0 * k0 * g00 + k0 * (mixed + k1) * g01 + k0 * k1 * g02 + k1 * mixed * g11
    a1 = rr1 / (curvature + k1 * k1 * g12)
    u0, u1 = got(4), got(5)
    place = (slot_column - 1.0 == iota((2 * tiles, COLS), 1).astype(f32)).astype(bf16)
    for out, slots in (
        (increment, (a0 + a1 * k0) * u0 + a1 * k1 * u1),
        (residual, (keep - a1 * k0) * u0 - (a0 + a1 * mixed) * u1 - a1 * k1 * u2),
    ):
        turned = jnp.concatenate([slots[0:tiles, :].T, slots[tiles:, :].T], axis=1)
        high, low = split(turned)
        field = nn(jnp.concatenate([high, low], axis=0), place)
        field = field[0 : 2 * SLAB, :] + field[2 * SLAB :, :]
        out[:, 0, :] = field[0:band, :]
        out[:, 1, :] = field[SLAB : SLAB + band, :]
    for use in range(7):
        left(use)


def shards(
    tiles,
    bands,
    jacobian,
    obs_tile,
    obs_column,
    obs_weight,
    innovation,
    precision_off,
    vertical_factor,
):
    obs, variables, band, channels = jacobian.shape
    f32, bf16 = jnp.float32, jnp.bfloat16
    meta = jnp.concatenate(
        [obs_tile.astype(f32), obs_column.astype(f32)[:, None], obs_weight[:, None]], axis=1
    )
    vmem = pl.BlockSpec(memory_space=pltpu.VMEM)
    out = jax.ShapeDtypeStruct((band, variables, COLS), f32)
    dma = pltpu.SemaphoreType.DMA
    return pl.pallas_call(
        functools.partial(kernel, tiles, bands),
        out_shape=(out, out),
        in_specs=[vmem] * 5,
        out_specs=(vmem, vmem),
        scratch_shapes=[
            pltpu.VMEM((obs * variables * SLAB, channels), bf16),
            pltpu.VMEM((channels, channels), f32),
            pltpu.VMEM((4 * SLAB, bands * ROWS), f32),
            pltpu.VMEM((obs, 2 * tiles), bf16),
            pltpu.VMEM((2 * tiles, 2 * obs), bf16),
            pltpu.VMEM((2 * tiles, 2 * tiles), bf16),
            pltpu.VMEM((3, bands, ROWS, 2 * obs), f32),
            pltpu.VMEM((2, bands, obs, channels), f32),
            pltpu.VMEM((7, tiles, 2, 2 * SLAB), f32),
            pltpu.VMEM((7, tiles, 2, 2 * SLAB), f32),
            pltpu.VMEM((obs, channels), f32),
            pltpu.VMEM((obs, channels), f32),
            pltpu.VMEM((obs, channels), f32),
            pltpu.VMEM((obs, channels), f32),
            dma((3, bands)),
            dma((3, bands)),
            dma((2, bands)),
            dma((2, bands)),
            dma((7,)),
            dma((7,)),
        ],
        compiler_params=pltpu.CompilerParams(
            collective_id=0, has_side_effects=True, vmem_limit_bytes=48 << 20
        ),
        name="analysis",
    )(
        jacobian.reshape(obs * variables, band, channels),
        meta,
        innovation,
        precision_off,
        vertical_factor,
    )


def solution(mesh):
    return jax.shard_map(
        functools.partial(shards, mesh.shape["horiz"], mesh.shape["lev"]),
        mesh=mesh,
        in_specs=(
            P("horiz", None, "lev", None),
            P("horiz", None),
            P("horiz"),
            P("horiz"),
            P("horiz", None),
            P(),
            P(),
        ),
        out_specs=(P("lev", None, "horiz"), P("lev", None, "horiz")),
        check_vma=False,
    )
```

```python
import functools

import jax
import jax.numpy as jnp
from jax import lax
from jax.experimental import pallas as pl
from jax.experimental.pallas import tpu as pltpu
from jax.sharding import PartitionSpec as P

MESH = pl.DeviceIdType.MESH
HIGHEST = lax.Precision.HIGHEST
COLS = 512
LANES = 128
SLAB = 80
HALF = SLAB // 2
GROUP = 8
COL_LANE = 127
SUM_LANE = 100
RING = 8
CORES = 2


def nt(a, b, precision=None):
    return lax.dot_general(
        a, b, (((1,), (1,)), ((), ())), precision=precision, preferred_element_type=jnp.float32
    )


def nn(a, b, precision=None):
    return lax.dot_general(
        a, b, (((1,), (0,)), ((), ())), precision=precision, preferred_element_type=jnp.float32
    )


def split(x):
    high = x.astype(jnp.bfloat16)
    return high, (x - high.astype(jnp.float32)).astype(jnp.bfloat16)


def iota(shape, dim):
    return lax.broadcasted_iota(jnp.int32, shape, dim)


def far_first(j):
    return lax.rem(RING // 2 + (1 - 2 * lax.rem(j, 2)) * ((j + 1) // 2) + RING, RING)


def for_peers(me, tiles, body):
    here_z, here_y, here_core = me // (RING * CORES), lax.rem(me // CORES, RING), lax.rem(me, CORES)

    @pl.loop(0, tiles - 1)
    def _(k):
        step = k // CORES
        z = lax.rem(here_z + far_first(step // RING), RING)
        y = lax.rem(here_y + far_first(lax.rem(step, RING)), RING)
        core = lax.rem(here_core + 1 + lax.rem(k, CORES), CORES)
        body((z * RING + y) * CORES + core)


def kernel(
    tiles,
    bands,
    jac,
    tile_in,
    column_in,
    weight_in,
    innovation_in,
    precision_in,
    vertical_in,
    increment,
    residual,
    jraw,
    tile_row,
    column_row,
    weight_row,
    innovation,
    precision_off,
    vertical,
    jpad,
    rmat,
    coef_high,
    coef_low,
    picks,
    sends,
    equal,
    repeat,
    tbuf,
    ibuf,
    sbuf,
    rbuf,
    w0_buf,
    im0_buf,
    w1_buf,
    in_sem,
    t_send,
    t_recv,
    i_send,
    i_recv,
    s_send,
    s_recv,
):
    me = lax.axis_index("horiz")
    lev = lax.axis_index("lev")
    obs, channels = innovation.shape
    band = jac.shape[1]
    levels = vertical.shape[1]
    used = 2 * band
    f32, bf16 = jnp.float32, jnp.bfloat16

    fetches = [
        pltpu.make_async_copy(source, target, in_sem.at[at])
        for at, (source, target) in enumerate(
            (
                (innovation_in, innovation),
                (precision_in, precision_off),
                (weight_in, weight_row),
                (tile_in, tile_row),
                (column_in, column_row),
                (jac, jraw),
                (vertical_in, vertical),
            )
        )
    ]
    for fetch in fetches:
        fetch.start()
    barrier = pltpu.get_barrier_semaphore()
    for k in range(1, bands):
        peer = lax.rem(lev + k, bands)
        pl.semaphore_signal(barrier, inc=1, device_id={"lev": peer}, device_id_type=MESH)

    def greet(peer):
        pl.semaphore_signal(barrier, inc=1, device_id={"horiz": peer}, device_id_type=MESH)

    for_peers(me, tiles, greet)

    def column(row):
        return jnp.broadcast_to(row[...].astype(f32), (obs, obs)).T[:, 0:1]

    for fetch in fetches[:5]:
        fetch.wait()
    weight = column(weight_row)
    off = precision_off[...]
    eye_c = (iota((channels, channels), 0) == iota((channels, channels), 1)).astype(f32)
    rmat[...] = eye_c + 0.5 * (off + off.T)

    def weigh(values):
        return weight * nn(values, rmat[...], HIGHEST)

    w0 = weigh(innovation[...]).astype(bf16)
    w0_buf[...] = w0.astype(f32)

    fetches[5].wait()

    @pl.loop(0, obs, unroll=4)
    def _(o):
        start = pl.multiple_of(o * SLAB, 16)
        jpad[pl.ds(start + 64, 16), :] = jnp.zeros((16, channels), bf16)
        jpad[pl.ds(start, used), :] = jraw[o].reshape(used, channels)

    def adjoint(use, high, low):
        both = jnp.concatenate([high, low], axis=0)
        lane = lax.rem(iota((SLAB, 2 * obs), 1), obs)

        def step(g, total):
            start = pl.multiple_of(g * (GROUP * SLAB), 16)
            product = nt(jpad[pl.ds(start, GROUP * SLAB), :], both)
            for j in range(GROUP):
                mine = lane == g * GROUP + j
                total = total + jnp.where(mine, product[j * SLAB : (j + 1) * SLAB, :], 0.0)
            return total

        t = lax.fori_loop(0, obs // GROUP, step, jnp.zeros((SLAB, 2 * obs), f32), unroll=8)
        t = t + pltpu.roll(t, obs, 1)
        tbuf[use, lev] = jnp.where(iota((HALF, 2 * obs), 1) < obs, t[0:HALF, :], t[HALF:, :])

    adjoint(0, w0, jnp.zeros_like(w0))

    onehot = (column(tile_row) == iota((obs, tiles), 1).astype(f32)).astype(f32)
    same = nt(onehot.astype(bf16), onehot.astype(bf16))
    earlier = iota((obs, obs), 1) < iota((obs, obs), 0)
    position = jnp.sum(jnp.where(earlier, same, 0.0), axis=1, keepdims=True)
    first = jnp.where(position < 0.5, onehot, 0.0)
    second = jnp.where(position > 0.5, onehot, 0.0)
    picks[:, 0:tiles] = first.astype(bf16)
    picks[:, tiles : 2 * tiles] = second.astype(bf16)
    nothing = jnp.zeros((obs, tiles), f32)
    sends[0:tiles, :] = jnp.concatenate([first, nothing], axis=0).T.astype(bf16)
    sends[tiles : 2 * tiles, :] = jnp.concatenate([second, nothing], axis=0).T.astype(bf16)
    repeat[...] = (
        iota((LANES, GROUP * SLAB), 0) == lax.rem(iota((LANES, GROUP * SLAB), 1), SLAB)
    ).astype(bf16)

    fetches[6].wait()

    row = iota((LANES, levels), 0)
    wide = iota((levels, 2 * bands * HALF), 1)
    places = lax.rem(wide, HALF) + (wide // (bands * HALF)) * HALF
    wide_level = lax.rem(wide // HALF, bands) * band + places // 2
    inside = (places < used) & (wide_level == iota(wide.shape, 0))
    eye_l = (iota((levels, levels), 0) == iota((levels, levels), 1)).astype(f32)
    both, back = 0.0, 0.0
    for v in range(2):
        factor = eye_l + vertical[v]
        own = (iota(row.shape, 1) == lev * band + row // 2) & (row < used) & (lax.rem(row, 2) == v)
        spread = jnp.where(inside & (lax.rem(places, 2) == v), 1.0, 0.0)
        own = own.astype(f32)
        both = both + nn(nt(nn(own, factor, HIGHEST), factor, HIGHEST), spread, HIGHEST)
        back = back + nn(nt(own, factor, HIGHEST), spread, HIGHEST)
    coef_high[0:LANES, :], coef_low[0:LANES, :] = split(both)
    coef_high[LANES:, :], coef_low[LANES:, :] = split(back)

    def band_copies(buf, use, send_sem, recv_sem, part, rows):
        copies = []
        for k in range(1, bands):
            copy = pltpu.make_async_remote_copy(
                src_ref=buf.at[use, lev, rows],
                dst_ref=buf.at[use, lev, rows],
                send_sem=send_sem.at[use, part, k],
                recv_sem=recv_sem.at[use, part, k],
                device_id={"lev": lax.rem(lev + k, bands)},
                device_id_type=MESH,
            )
            copy.start()
            copies.append(copy)
        return copies

    def gather_bands(use):
        return band_copies(tbuf, use, t_send, t_recv, 0, pl.ds(0, HALF))

    def columns(use, part):
        gathered = tbuf[use].reshape(bands * HALF, 2 * obs)
        gathered = jnp.concatenate([gathered, pltpu.roll(gathered, obs, 1)], axis=0)
        high, low = split(gathered)
        rows = pl.ds(part * LANES, LANES)
        mapped = nn(coef_high[rows, :], high) + (
            nn(coef_high[rows, :], low) + nn(coef_low[rows, :], high)
        )
        mapped = jnp.where(iota((LANES, 2 * obs), 1) < obs, mapped, 0.0)
        high, low = split(mapped)
        slots = nt(sends[...], jnp.concatenate([high, low], axis=0))
        return slots[:, 0:LANES] + slots[:, LANES:]

    def exchange(use):
        def send(peer):
            pltpu.make_async_remote_copy(
                src_ref=sbuf.at[use, peer],
                dst_ref=rbuf.at[use, me],
                send_sem=s_send.at[use],
                recv_sem=s_recv.at[use],
                device_id={"horiz": peer},
                device_id_type=MESH,
            ).start()

        for_peers(me, tiles, send)
        rbuf[use, me] = sbuf[use, me]

    def arrived(use):
        part = rbuf.at[use, pl.ds(0, tiles - 1)]
        pltpu.make_async_copy(part, part, s_recv.at[use]).wait()

    def left(use):
        part = sbuf.at[use, pl.ds(0, tiles - 1)]
        pltpu.make_async_copy(part, part, s_send.at[use]).wait()

    def put(use, slots):
        sbuf[use, :, 0, :] = slots[0:tiles, :]
        sbuf[use, :, 1, :] = slots[tiles : 2 * tiles, :]

    def got(use):
        return jnp.concatenate([rbuf[use, :, 0, :], rbuf[use, :, 1, :]], axis=0)

    def sum_at_tiles(use, first_time):
        slots = got(use)
        if first_time:
            ids = [slots[s * tiles : (s + 1) * tiles, COL_LANE : COL_LANE + 1] for s in range(2)]
            wide = [jnp.broadcast_to(one, (tiles, tiles)) for one in ids]
            tall = [one.T for one in wide]
            for a in range(2):
                for b in range(2):
                    equal[a * tiles : (a + 1) * tiles, b * tiles : (b + 1) * tiles] = jnp.where(
                        (wide[a] == tall[b]) & (wide[a] > 0.5), 1.0, 0.0
                    ).astype(bf16)
        high, low = split(slots)
        sums = nn(equal[...], jnp.concatenate([high, low], axis=1))
        put(use + 1, sums[:, 0:LANES] + sums[:, LANES:])
        return slots

    def images(use, from_use):
        high, low = split(got(from_use))
        chosen = nn(picks[...], jnp.concatenate([high, low], axis=1)).astype(bf16)
        chosen = jnp.concatenate([chosen[:, 0:LANES], chosen[:, LANES:]], axis=0)
        spread = nn(chosen, repeat[...])
        shape = (2 * obs, GROUP * SLAB)
        spread = jnp.where(lax.rem(iota(shape, 0), GROUP) == iota(shape, 1) // SLAB, spread, 0.0)
        copies = []
        half = obs // GROUP // 2
        for g in range(obs // GROUP):
            at = g * GROUP
            lhs = jnp.concatenate(
                [spread[at : at + GROUP, :], spread[obs + at : obs + at + GROUP, :]], axis=0
            )
            part = nn(lhs.astype(bf16), jpad[at * SLAB : (at + GROUP) * SLAB, :])
            ibuf[use, lev, at : at + GROUP, :] = part[0:GROUP, :] + part[GROUP:, :]
            if g == half - 1 or g == 2 * half - 1:
                p = g // half
                rows = pl.ds(p * half * GROUP, half * GROUP)
                copies += band_copies(ibuf, use, i_send, i_recv, p, rows)
        for copy in copies:
            copy.wait()
        total = ibuf[use, 0]
        for m in range(1, bands):
            total = total + ibuf[use, m]
        return total

    def wait_all(copies):
        for copy in copies:
            copy.wait()

    pl.semaphore_wait(barrier, tiles - 1 + bands - 1)
    copies = gather_bands(0)
    column_rhs = jnp.concatenate([column(column_row) + 1.0, jnp.zeros((obs, 1), f32)], axis=0)
    column_rhs = jnp.where(iota((2 * obs, LANES), 1) == COL_LANE, column_rhs, 0.0)
    high, low = split(column_rhs)
    column_slots = nn(sends[...], high) + nn(sends[...], low)
    wait_all(copies)
    put(0, columns(0, 0) + column_slots)
    exchange(0)
    put(4, columns(0, 1))
    arrived(0)
    first_slots = sum_at_tiles(0, True)
    exchange(1)
    exchange(4)
    slot_column = first_slots[:, COL_LANE : COL_LANE + 1]
    arrived(1)
    im0 = images(0, 1)
    im0_buf[...] = im0
    w1 = weigh(im0)
    w1_buf[...] = w1
    adjoint(1, *split(w1))
    wait_all(gather_bands(1))
    put(2, columns(1, 0))
    exchange(2)
    put(5, columns(1, 1))
    arrived(2)
    sum_at_tiles(2, False)
    exchange(3)
    exchange(5)
    arrived(3)
    im1 = images(1, 3)
    w2 = weigh(im1)
    adjoint(2, *split(w2))
    copies = gather_bands(2)

    w0, im0, w1 = w0_buf[...], im0_buf[...], w1_buf[...]
    lane = iota((1, LANES), 1)
    scalars = jnp.zeros((1, LANES), f32)
    for at, (a, b) in enumerate(((w0, im0), (w1, im0), (w1, im1), (w2, im0), (w2, im1))):
        one = jnp.sum(jnp.sum(a * b, axis=1, keepdims=True), axis=0, keepdims=True)
        scalars = scalars + jnp.where(lane == SUM_LANE + at, one, 0.0)
    wait_all(copies)
    put(6, columns(2, 1) + scalars)
    exchange(6)

    place = (slot_column - 1.0 == iota((2 * tiles, COLS), 1).astype(f32)).astype(bf16)

    def field(slots):
        turned = jnp.concatenate([slots[0:tiles, :].T, slots[tiles:, :].T], axis=1)
        high, low = split(turned[0:SLAB, :])
        out = nn(jnp.concatenate([high, low], axis=0), place)
        return out[0:used, :] + out[SLAB : SLAB + used, :]

    arrived(4)
    increment[...] = field(got(4))
    arrived(5)
    residual[...] = field(got(5))
    arrived(6)
    last = got(6)
    sums = jnp.sum(last[0:tiles, :], axis=0, keepdims=True)
    g00, g01, g11, g02, g12 = (
        jnp.sum(jnp.where(lane == SUM_LANE + at, sums, 0.0), axis=1, keepdims=True)
        for at in range(5)
    )
    a0 = g00 / (g00 + g01)
    keep = 1.0 - a0
    rr1 = keep * keep * g00 - 2.0 * a0 * keep * g01 + a0 * a0 * g11
    k0 = keep + rr1 / g00
    k1 = -a0
    mixed = k0 + k1
    curvature = k0 * k0 * g00 + k0 * (mixed + k1) * g01 + k0 * k1 * g02 + k1 * mixed * g11
    a1 = rr1 / (curvature + k1 * k1 * g12)
    v0, v1, v2 = increment[...], residual[...], field(last)
    increment[...] = (a0 + a1 * k0) * v0 + a1 * k1 * v1
    residual[...] = (keep - a1 * k0) * v0 - (a0 + a1 * mixed) * v1 - a1 * k1 * v2
    for use in range(7):
        left(use)


def shards(
    tiles,
    bands,
    jacobian,
    obs_tile,
    obs_column,
    obs_weight,
    innovation,
    precision_off,
    vertical_factor,
):
    obs, variables, band, channels = jacobian.shape
    f32, bf16 = jnp.float32, jnp.bfloat16
    vmem = pl.BlockSpec(memory_space=pltpu.VMEM)
    out = jax.ShapeDtypeStruct((band * variables, COLS), f32)
    dma = pltpu.SemaphoreType.DMA
    by_level = jnp.transpose(jacobian, (0, 2, 1, 3))
    increment, residual = pl.pallas_call(
        functools.partial(kernel, tiles, bands),
        out_shape=(out, out),
        in_specs=[pl.BlockSpec(memory_space=pl.ANY)] * 7,
        out_specs=(vmem, vmem),
        scratch_shapes=[
            pltpu.VMEM(by_level.shape, bf16),
            pltpu.VMEM((1, obs), jnp.int32),
            pltpu.VMEM((1, obs), jnp.int32),
            pltpu.VMEM((1, obs), f32),
            pltpu.VMEM((obs, channels), f32),
            pltpu.VMEM((channels, channels), f32),
            pltpu.VMEM(vertical_factor.shape, f32),
            pltpu.VMEM((obs * SLAB, channels), bf16),
            pltpu.VMEM((channels, channels), f32),
            pltpu.VMEM((2 * LANES, 2 * bands * HALF), bf16),
            pltpu.VMEM((2 * LANES, 2 * bands * HALF), bf16),
            pltpu.VMEM((obs, 2 * tiles), bf16),
            pltpu.VMEM((2 * tiles, 2 * obs), bf16),
            pltpu.VMEM((2 * tiles, 2 * tiles), bf16),
            pltpu.VMEM((LANES, GROUP * SLAB), bf16),
            pltpu.VMEM((3, bands, HALF, 2 * obs), f32),
            pltpu.VMEM((2, bands, obs, channels), f32),
            pltpu.VMEM((7, tiles, 2, LANES), f32),
            pltpu.VMEM((7, tiles, 2, LANES), f32),
            pltpu.VMEM((obs, channels), f32),
            pltpu.VMEM((obs, channels), f32),
            pltpu.VMEM((obs, channels), f32),
            dma((7,)),
            dma((3, 1, bands)),
            dma((3, 1, bands)),
            dma((2, 2, bands)),
            dma((2, 2, bands)),
            dma((7,)),
            dma((7,)),
        ],
        compiler_params=pltpu.CompilerParams(
            collective_id=0, has_side_effects=True, vmem_limit_bytes=60 << 20
        ),
        name="analysis",
    )(
        by_level,
        obs_tile.reshape(1, obs),
        obs_column.reshape(1, obs),
        obs_weight.reshape(1, obs),
        innovation,
        precision_off,
        vertical_factor,
    )
    shape = (band, variables, COLS)
    return increment.reshape(shape), residual.reshape(shape)


def solution(mesh):
    return jax.shard_map(
        functools.partial(shards, mesh.shape["horiz"], mesh.shape["lev"]),
        mesh=mesh,
        in_specs=(
            P("horiz", None, "lev", None),
            P("horiz", None),
            P("horiz"),
            P("horiz"),
            P("horiz", None),
            P(),
            P(),
        ),
        out_specs=(P("lev", None, "horiz"), P("lev", None, "horiz")),
        check_vma=False,
    )
```

```python
import functools

import jax
import jax.numpy as jnp
from jax import lax
from jax.experimental import pallas as pl
from jax.experimental.pallas import tpu as pltpu
from jax.sharding import PartitionSpec as P

MESH = pl.DeviceIdType.MESH
HIGHEST = lax.Precision.HIGHEST
COLS = 512
LANES = 128
SLAB = 80
HALF = SLAB // 2
GROUP = 8
COL_LANE = 127
SUM_LANE = 100


def nt(a, b, precision=None):
    return lax.dot_general(
        a, b, (((1,), (1,)), ((), ())), precision=precision, preferred_element_type=jnp.float32
    )


def nn(a, b, precision=None):
    return lax.dot_general(
        a, b, (((1,), (0,)), ((), ())), precision=precision, preferred_element_type=jnp.float32
    )


def split(x):
    high = x.astype(jnp.bfloat16)
    return high, (x - high.astype(jnp.float32)).astype(jnp.bfloat16)


def iota(shape, dim):
    return lax.broadcasted_iota(jnp.int32, shape, dim)


def for_peers(me, tiles, body):
    half = tiles // 2
    body(lax.rem(me + half, tiles))

    @pl.loop(1, half)
    def _(k):
        body(lax.rem(me + (half + k), tiles))
        body(lax.rem(me + (half - k), tiles))


def kernel(
    tiles,
    bands,
    jac,
    tile_in,
    column_in,
    weight_in,
    innovation_in,
    precision_in,
    vertical_in,
    increment,
    residual,
    jraw,
    tile_row,
    column_row,
    weight_row,
    innovation,
    precision_off,
    vertical,
    jpad,
    rmat,
    coef_high,
    coef_low,
    picks,
    sends,
    equal,
    repeat,
    tbuf,
    ibuf,
    sbuf,
    rbuf,
    w_buf,
    im_buf,
    fields,
    in_sem,
    t_send,
    t_recv,
    i_send,
    i_recv,
    s_send,
    s_recv,
):
    me = lax.axis_index("horiz")
    lev = lax.axis_index("lev")
    obs, channels = innovation.shape
    band = jac.shape[1]
    levels = vertical.shape[1]
    used = 2 * band
    f32, bf16 = jnp.float32, jnp.bfloat16

    fetches = [
        pltpu.make_async_copy(source, target, in_sem.at[at])
        for at, (source, target) in enumerate(
            (
                (innovation_in, innovation),
                (precision_in, precision_off),
                (weight_in, weight_row),
                (tile_in, tile_row),
                (column_in, column_row),
                (jac, jraw),
                (vertical_in, vertical),
            )
        )
    ]
    for fetch in fetches:
        fetch.start()
    barrier = pltpu.get_barrier_semaphore()
    for k in range(1, bands):
        peer = lax.rem(lev + k, bands)
        pl.semaphore_signal(barrier, inc=1, device_id={"lev": peer}, device_id_type=MESH)

    def greet(peer):
        pl.semaphore_signal(barrier, inc=1, device_id={"horiz": peer}, device_id_type=MESH)

    for_peers(me, tiles, greet)

    def column(row):
        return jnp.broadcast_to(row[...].astype(f32), (obs, obs)).T[:, 0:1]

    for fetch in fetches[:5]:
        fetch.wait()
    weight = column(weight_row)
    off = precision_off[...]
    eye_c = (iota((channels, channels), 0) == iota((channels, channels), 1)).astype(f32)
    rmat[...] = eye_c + 0.5 * (off + off.T)

    w0 = (weight * nn(innovation[...], rmat[...], HIGHEST)).astype(bf16)
    w_buf[0] = w0.astype(f32)

    fetches[5].wait()

    @pl.loop(0, obs, unroll=4)
    def _(o):
        start = pl.multiple_of(o * SLAB, 16)
        jpad[pl.ds(start + 64, 16), :] = jnp.zeros((16, channels), bf16)
        jpad[pl.ds(start, used), :] = jraw[o].reshape(used, channels)

    def adjoint(high, low, part, parts, total):
        groups = obs // GROUP // parts
        rows = groups * GROUP
        before = [jnp.zeros((rows, channels), bf16)] * part
        after = [jnp.zeros((rows, channels), bf16)] * (parts - 1 - part)
        both = jnp.concatenate([*before, high, *after, *before, low, *after], axis=0)
        lane = lax.rem(iota((SLAB, 2 * obs), 1), obs)
        for g in range(part * groups, (part + 1) * groups):
            product = nt(jpad[g * GROUP * SLAB : (g + 1) * GROUP * SLAB, :], both)
            for j in range(GROUP):
                mine = lane == g * GROUP + j
                total = total + jnp.where(mine, product[j * SLAB : (j + 1) * SLAB, :], 0.0)
        return total

    def store_terms(use, t):
        t = t + pltpu.roll(t, obs, 1)
        tbuf[use, lev] = jnp.where(iota((HALF, 2 * obs), 1) < obs, t[0:HALF, :], t[HALF:, :])

    no_terms = jnp.zeros((SLAB, 2 * obs), f32)
    store_terms(0, adjoint(w0, jnp.zeros_like(w0), 0, 1, no_terms))

    def band_copies(buf, use, send_sem, recv_sem, part, rows):
        copies = []
        for k in range(1, bands):
            copy = pltpu.make_async_remote_copy(
                src_ref=buf.at[use, lev, rows],
                dst_ref=buf.at[use, lev, rows],
                send_sem=send_sem.at[use, part, k],
                recv_sem=recv_sem.at[use, part, k],
                device_id={"lev": lax.rem(lev + k, bands)},
                device_id_type=MESH,
            )
            copy.start()
            copies.append(copy)
        return copies

    def gather_bands(use):
        return band_copies(tbuf, use, t_send, t_recv, 0, pl.ds(0, HALF))

    pl.semaphore_wait(barrier, tiles - 1 + bands - 1)
    copies = gather_bands(0)

    onehot = (column(tile_row) == iota((obs, tiles), 1).astype(f32)).astype(f32)
    same = nt(onehot.astype(bf16), onehot.astype(bf16))
    earlier = iota((obs, obs), 1) < iota((obs, obs), 0)
    position = jnp.sum(jnp.where(earlier, same, 0.0), axis=1, keepdims=True)
    first = jnp.where(position < 0.5, onehot, 0.0)
    second = jnp.where(position > 0.5, onehot, 0.0)
    picks[:, 0:tiles] = first.astype(bf16)
    picks[:, tiles : 2 * tiles] = second.astype(bf16)
    nothing = jnp.zeros((obs, tiles), f32)
    sends[0:tiles, :] = jnp.concatenate([first, nothing], axis=0).T.astype(bf16)
    sends[tiles : 2 * tiles, :] = jnp.concatenate([second, nothing], axis=0).T.astype(bf16)
    repeat[...] = (
        iota((LANES, GROUP * SLAB), 0) == lax.rem(iota((LANES, GROUP * SLAB), 1), SLAB)
    ).astype(bf16)

    fetches[6].wait()

    row = iota((LANES, levels), 0)
    wide = iota((levels, 2 * bands * HALF), 1)
    places = lax.rem(wide, HALF) + (wide // (bands * HALF)) * HALF
    wide_level = lax.rem(wide // HALF, bands) * band + places // 2
    inside = (places < used) & (wide_level == iota(wide.shape, 0))
    eye_l = (iota((levels, levels), 0) == iota((levels, levels), 1)).astype(f32)
    both, back = 0.0, 0.0
    for v in range(2):
        factor = eye_l + vertical[v]
        own = (iota(row.shape, 1) == lev * band + row // 2) & (row < used) & (lax.rem(row, 2) == v)
        spread = jnp.where(inside & (lax.rem(places, 2) == v), 1.0, 0.0)
        own = own.astype(f32)
        both = both + nn(nt(nn(own, factor, HIGHEST), factor, HIGHEST), spread, HIGHEST)
        back = back + nn(nt(own, factor, HIGHEST), spread, HIGHEST)
    coef_high[0:LANES, :], coef_low[0:LANES, :] = split(both)
    coef_high[LANES:, :], coef_low[LANES:, :] = split(back)

    def columns(use, part):
        gathered = tbuf[use].reshape(bands * HALF, 2 * obs)
        gathered = jnp.concatenate([gathered, pltpu.roll(gathered, obs, 1)], axis=0)
        high, low = split(gathered)
        rows = pl.ds(part * LANES, LANES)
        mapped = nn(coef_high[rows, :], high) + (
            nn(coef_high[rows, :], low) + nn(coef_low[rows, :], high)
        )
        mapped = jnp.where(iota((LANES, 2 * obs), 1) < obs, mapped, 0.0)
        high, low = split(mapped)
        slots = nt(sends[...], jnp.concatenate([high, low], axis=0))
        return slots[:, 0:LANES] + slots[:, LANES:]

    def exchange(use):
        def send(peer):
            pltpu.make_async_remote_copy(
                src_ref=sbuf.at[use, peer],
                dst_ref=rbuf.at[use, me],
                send_sem=s_send.at[use],
                recv_sem=s_recv.at[use],
                device_id={"horiz": peer},
                device_id_type=MESH,
            ).start()

        for_peers(me, tiles, send)
        rbuf[use, me] = sbuf[use, me]

    def arrived(use):
        part = rbuf.at[use, pl.ds(0, tiles - 1)]
        pltpu.make_async_copy(part, part, s_recv.at[use]).wait()

    def left(use):
        part = sbuf.at[use, pl.ds(0, tiles - 1)]
        pltpu.make_async_copy(part, part, s_send.at[use]).wait()

    def put(use, slots):
        sbuf[use, :, 0, :] = slots[0:tiles, :]
        sbuf[use, :, 1, :] = slots[tiles : 2 * tiles, :]

    def got(use):
        return jnp.concatenate([rbuf[use, :, 0, :], rbuf[use, :, 1, :]], axis=0)

    def sum_at_tiles(use, first_time):
        slots = got(use)
        if first_time:
            ids = [slots[s * tiles : (s + 1) * tiles, COL_LANE : COL_LANE + 1] for s in range(2)]
            wide = [jnp.broadcast_to(one, (tiles, tiles)) for one in ids]
            tall = [one.T for one in wide]
            for a in range(2):
                for b in range(2):
                    equal[a * tiles : (a + 1) * tiles, b * tiles : (b + 1) * tiles] = jnp.where(
                        (wide[a] == tall[b]) & (wide[a] > 0.5), 1.0, 0.0
                    ).astype(bf16)
        high, low = split(slots)
        sums = nn(equal[...], jnp.concatenate([high, low], axis=1))
        put(use + 1, sums[:, 0:LANES] + sums[:, LANES:])
        return slots

    parts = 2

    def start_images(use, from_use):
        high, low = split(got(from_use))
        chosen = nn(picks[...], jnp.concatenate([high, low], axis=1)).astype(bf16)
        chosen = jnp.concatenate([chosen[:, 0:LANES], chosen[:, LANES:]], axis=0)
        spread = nn(chosen, repeat[...])
        shape = (2 * obs, GROUP * SLAB)
        spread = jnp.where(lax.rem(iota(shape, 0), GROUP) == iota(shape, 1) // SLAB, spread, 0.0)
        copies = []
        groups = obs // GROUP // parts
        for g in range(obs // GROUP):
            at = g * GROUP
            lhs = jnp.concatenate(
                [spread[at : at + GROUP, :], spread[obs + at : obs + at + GROUP, :]], axis=0
            )
            part = nn(lhs.astype(bf16), jpad[at * SLAB : (at + GROUP) * SLAB, :])
            ibuf[use, lev, at : at + GROUP, :] = part[0:GROUP, :] + part[GROUP:, :]
            if (g + 1) % groups == 0:
                p = g // groups
                rows = pl.ds(p * groups * GROUP, groups * GROUP)
                copies.append(band_copies(ibuf, use, i_send, i_recv, p, rows))
        return copies

    def weigh_images(use, copies):
        terms = no_terms
        size = obs // parts
        for p in range(parts):
            wait_all(copies[p])
            rows = slice(p * size, (p + 1) * size)
            total = ibuf[use, 0, rows, :]
            for m in range(1, bands):
                total = total + ibuf[use, m, rows, :]
            im_buf[use, rows, :] = total
            w = weight[rows, :] * nn(total, rmat[...], HIGHEST)
            w_buf[use + 1, rows, :] = w
            high, low = split(w)
            terms = adjoint(high, low, p, parts, terms)
        store_terms(use + 1, terms)

    def wait_all(copies):
        for copy in copies:
            copy.wait()

    column_rhs = jnp.concatenate([column(column_row) + 1.0, jnp.zeros((obs, 1), f32)], axis=0)
    column_rhs = jnp.where(iota((2 * obs, LANES), 1) == COL_LANE, column_rhs, 0.0)
    high, low = split(column_rhs)
    column_slots = nn(sends[...], high) + nn(sends[...], low)
    wait_all(copies)
    put(0, columns(0, 0) + column_slots)
    exchange(0)
    put(4, columns(0, 1))
    arrived(0)
    first_slots = sum_at_tiles(0, True)
    exchange(1)
    slot_column = first_slots[:, COL_LANE : COL_LANE + 1]
    arrived(1)
    copies = start_images(0, 1)
    exchange(4)
    weigh_images(0, copies)
    wait_all(gather_bands(1))
    put(2, columns(1, 0))
    exchange(2)
    put(5, columns(1, 1))
    arrived(2)
    sum_at_tiles(2, False)
    exchange(3)
    arrived(3)
    copies = start_images(1, 3)
    exchange(5)
    weigh_images(1, copies)
    copies = gather_bands(2)

    w0, w1, w2 = w_buf[0], w_buf[1], w_buf[2]
    im0, im1 = im_buf[0], im_buf[1]
    lane = iota((1, LANES), 1)
    scalars = jnp.zeros((1, LANES), f32)
    for at, (a, b) in enumerate(((w0, im0), (w1, im0), (w1, im1), (w2, im0), (w2, im1))):
        one = jnp.sum(jnp.sum(a * b, axis=1, keepdims=True), axis=0, keepdims=True)
        scalars = scalars + jnp.where(lane == SUM_LANE + at, one, 0.0)
    wait_all(copies)
    put(6, columns(2, 1) + scalars)
    exchange(6)

    place = (slot_column - 1.0 == iota((2 * tiles, COLS), 1).astype(f32)).astype(bf16)

    def field(slots):
        turned = jnp.concatenate([slots[0:tiles, :].T, slots[tiles:, :].T], axis=1)
        high, low = split(turned[0:SLAB, :])
        out = nn(jnp.concatenate([high, low], axis=0), place)
        return out[0:used, :] + out[SLAB : SLAB + used, :]

    arrived(4)
    fields[0] = field(got(4))
    arrived(5)
    fields[1] = field(got(5))
    arrived(6)
    last = got(6)
    sums = jnp.sum(last[0:tiles, :], axis=0, keepdims=True)
    g00, g01, g11, g02, g12 = (
        jnp.sum(jnp.where(lane == SUM_LANE + at, sums, 0.0), axis=1, keepdims=True)
        for at in range(5)
    )
    a0 = g00 / (g00 + g01)
    keep = 1.0 - a0
    rr1 = keep * keep * g00 - 2.0 * a0 * keep * g01 + a0 * a0 * g11
    k0 = keep + rr1 / g00
    k1 = -a0
    mixed = k0 + k1
    curvature = k0 * k0 * g00 + k0 * (mixed + k1) * g01 + k0 * k1 * g02 + k1 * mixed * g11
    a1 = rr1 / (curvature + k1 * k1 * g12)
    v0, v1, v2 = fields[0], fields[1], field(last)
    shape = increment.shape
    increment[...] = ((a0 + a1 * k0) * v0 + a1 * k1 * v1).reshape(shape)
    residual[...] = (
        (keep - a1 * k0) * v0 - (a0 + a1 * mixed) * v1 - a1 * k1 * v2
    ).reshape(shape)
    for use in range(7):
        left(use)


def shards(
    tiles,
    bands,
    jacobian,
    obs_tile,
    obs_column,
    obs_weight,
    innovation,
    precision_off,
    vertical_factor,
):
    obs, variables, band, channels = jacobian.shape
    f32, bf16 = jnp.float32, jnp.bfloat16
    vmem = pl.BlockSpec(memory_space=pltpu.VMEM)
    out = jax.ShapeDtypeStruct((band, variables, COLS), f32)
    dma = pltpu.SemaphoreType.DMA
    by_level = jnp.transpose(jacobian, (0, 2, 1, 3))
    increment, residual = pl.pallas_call(
        functools.partial(kernel, tiles, bands),
        out_shape=(out, out),
        in_specs=[pl.BlockSpec(memory_space=pl.ANY)] * 7,
        out_specs=(vmem, vmem),
        scratch_shapes=[
            pltpu.VMEM(by_level.shape, bf16),
            pltpu.VMEM((1, obs), jnp.int32),
            pltpu.VMEM((1, obs), jnp.int32),
            pltpu.VMEM((1, obs), f32),
            pltpu.VMEM((obs, channels), f32),
            pltpu.VMEM((channels, channels), f32),
            pltpu.VMEM(vertical_factor.shape, f32),
            pltpu.VMEM((obs * SLAB, channels), bf16),
            pltpu.VMEM((channels, channels), f32),
            pltpu.VMEM((2 * LANES, 2 * bands * HALF), bf16),
            pltpu.VMEM((2 * LANES, 2 * bands * HALF), bf16),
            pltpu.VMEM((obs, 2 * tiles), bf16),
            pltpu.VMEM((2 * tiles, 2 * obs), bf16),
            pltpu.VMEM((2 * tiles, 2 * tiles), bf16),
            pltpu.VMEM((LANES, GROUP * SLAB), bf16),
            pltpu.VMEM((3, bands, HALF, 2 * obs), f32),
            pltpu.VMEM((2, bands, obs, channels), f32),
            pltpu.VMEM((7, tiles, 2, LANES), f32),
            pltpu.VMEM((7, tiles, 2, LANES), f32),
            pltpu.VMEM((3, obs, channels), f32),
            pltpu.VMEM((2, obs, channels), f32),
            pltpu.VMEM((2, variables * band, COLS), f32),
            dma((7,)),
            dma((3, 1, bands)),
            dma((3, 1, bands)),
            dma((2, 2, bands)),
            dma((2, 2, bands)),
            dma((7,)),
            dma((7,)),
        ],
        compiler_params=pltpu.CompilerParams(
            collective_id=0, has_side_effects=True, vmem_limit_bytes=60 << 20
        ),
        name="analysis",
    )(
        by_level,
        obs_tile.reshape(1, obs),
        obs_column.reshape(1, obs),
        obs_weight.reshape(1, obs),
        innovation,
        precision_off,
        vertical_factor,
    )
    return increment, residual


def solution(mesh):
    return jax.shard_map(
        functools.partial(shards, mesh.shape["horiz"], mesh.shape["lev"]),
        mesh=mesh,
        in_specs=(
            P("horiz", None, "lev", None),
            P("horiz", None),
            P("horiz"),
            P("horiz"),
            P("horiz", None),
            P(),
            P(),
        ),
        out_specs=(P("lev", None, "horiz"), P("lev", None, "horiz")),
        check_vma=False,
    )
```

```python
import functools

import jax
import jax.numpy as jnp
from jax import lax
from jax.experimental import pallas as pl
from jax.experimental.pallas import tpu as pltpu
from jax.sharding import PartitionSpec as P

MESH = pl.DeviceIdType.MESH
HIGHEST = lax.Precision.HIGHEST
COLS = 512
LANES = 128
SLAB = 80
HALF = SLAB // 2
GROUP = 8
RING = 8
CORES = 2
COL_LANE = 127
SUM_LANE = 100


def nt(a, b, precision=None):
    return lax.dot_general(
        a, b, (((1,), (1,)), ((), ())), precision=precision, preferred_element_type=jnp.float32
    )


def nn(a, b, precision=None):
    return lax.dot_general(
        a, b, (((1,), (0,)), ((), ())), precision=precision, preferred_element_type=jnp.float32
    )


def split(x):
    high = x.astype(jnp.bfloat16)
    return high, (x - high.astype(jnp.float32)).astype(jnp.bfloat16)


def iota(shape, dim):
    return lax.broadcasted_iota(jnp.int32, shape, dim)


def hops(offset):
    return min(offset, RING - offset)


def far_first():
    offsets = [(z, y) for z in range(RING) for y in range(RING)]
    return sorted(offsets, key=lambda at: -hops(at[0]) - hops(at[1]))


def for_peers(me, body):
    here_z, here_y, core = me // (RING * CORES), lax.rem(me // CORES, RING), lax.rem(me, CORES)
    at_z = [lax.rem(here_z + d, RING) * (RING * CORES) for d in range(RING)]
    at_y = [lax.rem(here_y + d, RING) * CORES for d in range(RING)]
    for z, y in far_first():
        chip = at_z[z] + at_y[y]
        for d in range(CORES):
            if z or y or d:
                body(chip + lax.rem(core + d, CORES))


def kernel(
    tiles,
    bands,
    jac,
    tile_in,
    column_in,
    weight_in,
    innovation_in,
    precision_in,
    vertical_in,
    increment,
    residual,
    jraw,
    tile_row,
    column_row,
    weight_row,
    innovation,
    precision_off,
    vertical,
    jpad,
    rmat,
    coef_high,
    coef_low,
    picks,
    sends,
    equal,
    repeat,
    tbuf,
    ibuf,
    sbuf,
    rbuf,
    w_buf,
    im_buf,
    fields,
    entered,
    in_sem,
    t_send,
    t_recv,
    i_send,
    i_recv,
    s_send,
    s_recv,
):
    me = lax.axis_index("horiz")
    lev = lax.axis_index("lev")
    obs, channels = innovation.shape
    band = jac.shape[1]
    levels = vertical.shape[1]
    used = 2 * band
    f32, bf16 = jnp.float32, jnp.bfloat16

    fetches = [
        pltpu.make_async_copy(source, target, in_sem.at[at])
        for at, (source, target) in enumerate(
            (
                (innovation_in, innovation),
                (precision_in, precision_off),
                (weight_in, weight_row),
                (tile_in, tile_row),
                (column_in, column_row),
                (jac, jraw),
                (vertical_in, vertical),
            )
        )
    ]
    for fetch in fetches:
        fetch.start()
    barrier = pltpu.get_barrier_semaphore()
    for k in range(1, bands):
        peer = lax.rem(lev + k, bands)
        pl.semaphore_signal(barrier, inc=1, device_id={"lev": peer}, device_id_type=MESH)

    def greet(semaphore, peer):
        pl.semaphore_signal(semaphore, inc=1, device_id={"horiz": peer}, device_id_type=MESH)

    plane = RING * CORES
    line_peers = [lax.rem(me + k * plane, tiles) for k in range(1, RING)]
    plane_peers = [me // plane * plane + lax.rem(me + k, plane) for k in range(1, plane)]
    for peer in line_peers + plane_peers:
        greet(barrier, peer)

    def column(row):
        return jnp.broadcast_to(row[...].astype(f32), (obs, obs)).T[:, 0:1]

    for fetch in fetches[:5]:
        fetch.wait()
    weight = column(weight_row)
    off = precision_off[...]
    eye_c = (iota((channels, channels), 0) == iota((channels, channels), 1)).astype(f32)
    rmat[...] = eye_c + 0.5 * (off + off.T)

    w0 = (weight * nn(innovation[...], rmat[...], HIGHEST)).astype(bf16)
    w_buf[0] = w0.astype(f32)

    fetches[5].wait()

    @pl.loop(0, obs, unroll=4)
    def _(o):
        start = pl.multiple_of(o * SLAB, 16)
        jpad[pl.ds(start + 64, 16), :] = jnp.zeros((16, channels), bf16)
        jpad[pl.ds(start, used), :] = jraw[o].reshape(used, channels)

    def adjoint(high, low, part, parts, total):
        groups = obs // GROUP // parts
        rows = groups * GROUP
        before = [jnp.zeros((rows, channels), bf16)] * part
        after = [jnp.zeros((rows, channels), bf16)] * (parts - 1 - part)
        both = jnp.concatenate([*before, high, *after, *before, low, *after], axis=0)
        lane = lax.rem(iota((SLAB, 2 * obs), 1), obs)
        for g in range(part * groups, (part + 1) * groups):
            product = nt(jpad[g * GROUP * SLAB : (g + 1) * GROUP * SLAB, :], both)
            for j in range(GROUP):
                mine = lane == g * GROUP + j
                total = total + jnp.where(mine, product[j * SLAB : (j + 1) * SLAB, :], 0.0)
        return total

    def store_terms(use, t):
        t = t + pltpu.roll(t, obs, 1)
        tbuf[use, lev] = jnp.where(iota((HALF, 2 * obs), 1) < obs, t[0:HALF, :], t[HALF:, :])

    no_terms = jnp.zeros((SLAB, 2 * obs), f32)
    store_terms(0, adjoint(w0, jnp.zeros_like(w0), 0, 1, no_terms))

    def band_copies(buf, use, send_sem, recv_sem, part, rows):
        copies = []
        for k in range(1, bands):
            copy = pltpu.make_async_remote_copy(
                src_ref=buf.at[use, lev, rows],
                dst_ref=buf.at[use, lev, rows],
                send_sem=send_sem.at[use, part, k],
                recv_sem=recv_sem.at[use, part, k],
                device_id={"lev": lax.rem(lev + k, bands)},
                device_id_type=MESH,
            )
            copy.start()
            copies.append(copy)
        return copies

    def gather_bands(use):
        return band_copies(tbuf, use, t_send, t_recv, 0, pl.ds(0, HALF))

    pl.semaphore_wait(barrier, bands - 1 + len(line_peers) + len(plane_peers))
    copies = gather_bands(0)
    for peer in plane_peers:
        greet(entered, peer)

    onehot = (column(tile_row) == iota((obs, tiles), 1).astype(f32)).astype(f32)
    same = nt(onehot.astype(bf16), onehot.astype(bf16))
    earlier = iota((obs, obs), 1) < iota((obs, obs), 0)
    position = jnp.sum(jnp.where(earlier, same, 0.0), axis=1, keepdims=True)
    first = jnp.where(position < 0.5, onehot, 0.0)
    second = jnp.where(position > 0.5, onehot, 0.0)
    picks[:, 0:tiles] = first.astype(bf16)
    picks[:, tiles : 2 * tiles] = second.astype(bf16)
    nothing = jnp.zeros((obs, tiles), f32)
    sends[0:tiles, :] = jnp.concatenate([first, nothing], axis=0).T.astype(bf16)
    sends[tiles : 2 * tiles, :] = jnp.concatenate([second, nothing], axis=0).T.astype(bf16)
    repeat[...] = (
        iota((LANES, GROUP * SLAB), 0) == lax.rem(iota((LANES, GROUP * SLAB), 1), SLAB)
    ).astype(bf16)

    fetches[6].wait()

    row = iota((LANES, levels), 0)
    wide = iota((levels, 2 * bands * HALF), 1)
    places = lax.rem(wide, HALF) + (wide // (bands * HALF)) * HALF
    wide_level = lax.rem(wide // HALF, bands) * band + places // 2
    inside = (places < used) & (wide_level == iota(wide.shape, 0))
    eye_l = (iota((levels, levels), 0) == iota((levels, levels), 1)).astype(f32)
    both, back = 0.0, 0.0
    for v in range(2):
        factor = eye_l + vertical[v]
        own = (iota(row.shape, 1) == lev * band + row // 2) & (row < used) & (lax.rem(row, 2) == v)
        spread = jnp.where(inside & (lax.rem(places, 2) == v), 1.0, 0.0)
        own = own.astype(f32)
        both = both + nn(nt(nn(own, factor, HIGHEST), factor, HIGHEST), spread, HIGHEST)
        back = back + nn(nt(own, factor, HIGHEST), spread, HIGHEST)
    coef_high[0:LANES, :], coef_low[0:LANES, :] = split(both)
    coef_high[LANES:, :], coef_low[LANES:, :] = split(back)

    def columns(use, part):
        gathered = tbuf[use].reshape(bands * HALF, 2 * obs)
        gathered = jnp.concatenate([gathered, pltpu.roll(gathered, obs, 1)], axis=0)
        high, low = split(gathered)
        rows = pl.ds(part * LANES, LANES)
        mapped = nn(coef_high[rows, :], high) + (
            nn(coef_high[rows, :], low) + nn(coef_low[rows, :], high)
        )
        mapped = jnp.where(iota((LANES, 2 * obs), 1) < obs, mapped, 0.0)
        high, low = split(mapped)
        slots = nt(sends[...], jnp.concatenate([high, low], axis=0))
        return slots[:, 0:LANES] + slots[:, LANES:]

    def exchange(use):
        def send(peer):
            pltpu.make_async_remote_copy(
                src_ref=sbuf.at[use, peer],
                dst_ref=rbuf.at[use, me],
                send_sem=s_send.at[use],
                recv_sem=s_recv.at[use],
                device_id={"horiz": peer},
                device_id_type=MESH,
            ).start()

        for_peers(me, send)
        rbuf[use, me] = sbuf[use, me]

    def arrived(use):
        part = rbuf.at[use, pl.ds(0, tiles - 1)]
        pltpu.make_async_copy(part, part, s_recv.at[use]).wait()

    def left(use):
        part = sbuf.at[use, pl.ds(0, tiles - 1)]
        pltpu.make_async_copy(part, part, s_send.at[use]).wait()

    def put(use, slots):
        sbuf[use, :, 0, :] = slots[0:tiles, :]
        sbuf[use, :, 1, :] = slots[tiles : 2 * tiles, :]

    def got(use):
        return jnp.concatenate([rbuf[use, :, 0, :], rbuf[use, :, 1, :]], axis=0)

    def sum_at_tiles(use, first_time):
        slots = got(use)
        if first_time:
            ids = [slots[s * tiles : (s + 1) * tiles, COL_LANE : COL_LANE + 1] for s in range(2)]
            wide = [jnp.broadcast_to(one, (tiles, tiles)) for one in ids]
            tall = [one.T for one in wide]
            for a in range(2):
                for b in range(2):
                    equal[a * tiles : (a + 1) * tiles, b * tiles : (b + 1) * tiles] = jnp.where(
                        (wide[a] == tall[b]) & (wide[a] > 0.5), 1.0, 0.0
                    ).astype(bf16)
        high, low = split(slots)
        sums = nn(equal[...], jnp.concatenate([high, low], axis=1))
        put(use + 1, sums[:, 0:LANES] + sums[:, LANES:])
        return slots

    parts = 2

    def start_images(use, from_use):
        high, low = split(got(from_use))
        chosen = nn(picks[...], jnp.concatenate([high, low], axis=1)).astype(bf16)
        chosen = jnp.concatenate([chosen[:, 0:LANES], chosen[:, LANES:]], axis=0)
        spread = nn(chosen, repeat[...])
        shape = (2 * obs, GROUP * SLAB)
        spread = jnp.where(lax.rem(iota(shape, 0), GROUP) == iota(shape, 1) // SLAB, spread, 0.0)
        copies = []
        groups = obs // GROUP // parts
        for g in range(obs // GROUP):
            at = g * GROUP
            lhs = jnp.concatenate(
                [spread[at : at + GROUP, :], spread[obs + at : obs + at + GROUP, :]], axis=0
            )
            part = nn(lhs.astype(bf16), jpad[at * SLAB : (at + GROUP) * SLAB, :])
            ibuf[use, lev, at : at + GROUP, :] = part[0:GROUP, :] + part[GROUP:, :]
            if (g + 1) % groups == 0:
                p = g // groups
                rows = pl.ds(p * groups * GROUP, groups * GROUP)
                copies.append(band_copies(ibuf, use, i_send, i_recv, p, rows))
        return copies

    def weigh_images(use, copies):
        terms = no_terms
        size = obs // parts
        for p in range(parts):
            wait_all(copies[p])
            rows = slice(p * size, (p + 1) * size)
            total = ibuf[use, 0, rows, :]
            for m in range(1, bands):
                total = total + ibuf[use, m, rows, :]
            im_buf[use, rows, :] = total
            w = weight[rows, :] * nn(total, rmat[...], HIGHEST)
            w_buf[use + 1, rows, :] = w
            high, low = split(w)
            terms = adjoint(high, low, p, parts, terms)
        store_terms(use + 1, terms)

    def wait_all(copies):
        for copy in copies:
            copy.wait()

    column_rhs = jnp.concatenate([column(column_row) + 1.0, jnp.zeros((obs, 1), f32)], axis=0)
    column_rhs = jnp.where(iota((2 * obs, LANES), 1) == COL_LANE, column_rhs, 0.0)
    high, low = split(column_rhs)
    column_slots = nn(sends[...], high) + nn(sends[...], low)
    wait_all(copies)
    put(0, columns(0, 0) + column_slots)
    pl.semaphore_wait(entered, len(plane_peers))
    exchange(0)
    put(4, columns(0, 1))
    arrived(0)
    first_slots = sum_at_tiles(0, True)
    exchange(1)
    slot_column = first_slots[:, COL_LANE : COL_LANE + 1]
    arrived(1)
    copies = start_images(0, 1)
    exchange(4)
    weigh_images(0, copies)
    wait_all(gather_bands(1))
    put(2, columns(1, 0))
    exchange(2)
    put(5, columns(1, 1))
    arrived(2)
    sum_at_tiles(2, False)
    exchange(3)
    arrived(3)
    copies = start_images(1, 3)
    exchange(5)
    weigh_images(1, copies)
    copies = gather_bands(2)

    w0, w1, w2 = w_buf[0], w_buf[1], w_buf[2]
    im0, im1 = im_buf[0], im_buf[1]
    lane = iota((1, LANES), 1)
    scalars = jnp.zeros((1, LANES), f32)
    for at, (a, b) in enumerate(((w0, im0), (w1, im0), (w1, im1), (w2, im0), (w2, im1))):
        one = jnp.sum(jnp.sum(a * b, axis=1, keepdims=True), axis=0, keepdims=True)
        scalars = scalars + jnp.where(lane == SUM_LANE + at, one, 0.0)
    wait_all(copies)
    put(6, columns(2, 1) + scalars)
    exchange(6)

    place = (slot_column - 1.0 == iota((2 * tiles, COLS), 1).astype(f32)).astype(bf16)

    def field(slots):
        turned = jnp.concatenate([slots[0:tiles, :].T, slots[tiles:, :].T], axis=1)
        high, low = split(turned[0:SLAB, :])
        out = nn(jnp.concatenate([high, low], axis=0), place)
        return out[0:used, :] + out[SLAB : SLAB + used, :]

    arrived(4)
    fields[0] = field(got(4))
    arrived(5)
    fields[1] = field(got(5))
    arrived(6)
    last = got(6)
    sums = jnp.sum(last[0:tiles, :], axis=0, keepdims=True)
    g00, g01, g11, g02, g12 = (
        jnp.sum(jnp.where(lane == SUM_LANE + at, sums, 0.0), axis=1, keepdims=True)
        for at in range(5)
    )
    a0 = g00 / (g00 + g01)
    keep = 1.0 - a0
    rr1 = keep * keep * g00 - 2.0 * a0 * keep * g01 + a0 * a0 * g11
    k0 = keep + rr1 / g00
    k1 = -a0
    mixed = k0 + k1
    curvature = k0 * k0 * g00 + k0 * (mixed + k1) * g01 + k0 * k1 * g02 + k1 * mixed * g11
    a1 = rr1 / (curvature + k1 * k1 * g12)
    v0, v1, v2 = fields[0], fields[1], field(last)
    shape = increment.shape
    increment[...] = ((a0 + a1 * k0) * v0 + a1 * k1 * v1).reshape(shape)
    residual[...] = (
        (keep - a1 * k0) * v0 - (a0 + a1 * mixed) * v1 - a1 * k1 * v2
    ).reshape(shape)
    for use in range(7):
        left(use)


def hand_on(a_in, b_in, a_out, b_out):
    a_out[...] = a_in[...]
    b_out[...] = b_in[...]


def shards(
    tiles,
    bands,
    jacobian,
    obs_tile,
    obs_column,
    obs_weight,
    innovation,
    precision_off,
    vertical_factor,
):
    obs, variables, band, channels = jacobian.shape
    f32, bf16 = jnp.float32, jnp.bfloat16
    vmem = pl.BlockSpec(memory_space=pltpu.VMEM)
    out = jax.ShapeDtypeStruct((band, variables, COLS), f32)
    dma = pltpu.SemaphoreType.DMA
    by_level = jnp.transpose(jacobian, (0, 2, 1, 3))
    increment, residual = pl.pallas_call(
        functools.partial(kernel, tiles, bands),
        out_shape=(out, out),
        in_specs=[pl.BlockSpec(memory_space=pl.ANY)] * 7,
        out_specs=(vmem, vmem),
        scratch_shapes=[
            pltpu.VMEM(by_level.shape, bf16),
            pltpu.VMEM((1, obs), jnp.int32),
            pltpu.VMEM((1, obs), jnp.int32),
            pltpu.VMEM((1, obs), f32),
            pltpu.VMEM((obs, channels), f32),
            pltpu.VMEM((channels, channels), f32),
            pltpu.VMEM(vertical_factor.shape, f32),
            pltpu.VMEM((obs * SLAB, channels), bf16),
            pltpu.VMEM((channels, channels), f32),
            pltpu.VMEM((2 * LANES, 2 * bands * HALF), bf16),
            pltpu.VMEM((2 * LANES, 2 * bands * HALF), bf16),
            pltpu.VMEM((obs, 2 * tiles), bf16),
            pltpu.VMEM((2 * tiles, 2 * obs), bf16),
            pltpu.VMEM((2 * tiles, 2 * tiles), bf16),
            pltpu.VMEM((LANES, GROUP * SLAB), bf16),
            pltpu.VMEM((3, bands, HALF, 2 * obs), f32),
            pltpu.VMEM((2, bands, obs, channels), f32),
            pltpu.VMEM((7, tiles, 2, LANES), f32),
            pltpu.VMEM((7, tiles, 2, LANES), f32),
            pltpu.VMEM((3, obs, channels), f32),
            pltpu.VMEM((2, obs, channels), f32),
            pltpu.VMEM((2, variables * band, COLS), f32),
            pltpu.SemaphoreType.REGULAR,
            dma((7,)),
            dma((3, 1, bands)),
            dma((3, 1, bands)),
            dma((2, 2, bands)),
            dma((2, 2, bands)),
            dma((7,)),
            dma((7,)),
        ],
        compiler_params=pltpu.CompilerParams(
            collective_id=0, has_side_effects=True, vmem_limit_bytes=60 << 20
        ),
        name="analysis",
    )(
        by_level,
        obs_tile.reshape(1, obs),
        obs_column.reshape(1, obs),
        obs_weight.reshape(1, obs),
        innovation,
        precision_off,
        vertical_factor,
    )
    return pl.pallas_call(
        hand_on,
        out_shape=(out, out),
        in_specs=[vmem] * 2,
        out_specs=[vmem] * 2,
        compiler_params=pltpu.CompilerParams(vmem_limit_bytes=60 << 20),
        name="outputs",
    )(increment, residual)


def solution(mesh):
    return jax.shard_map(
        functools.partial(shards, mesh.shape["horiz"], mesh.shape["lev"]),
        mesh=mesh,
        in_specs=(
            P("horiz", None, "lev", None),
            P("horiz", None),
            P("horiz"),
            P("horiz"),
            P("horiz", None),
            P(),
            P(),
        ),
        out_specs=(P("lev", None, "horiz"), P("lev", None, "horiz")),
        check_vma=False,
    )
```

```python
import functools

import jax
import jax.numpy as jnp
from jax import lax
from jax.experimental import pallas as pl
from jax.experimental.pallas import tpu as pltpu
from jax.sharding import PartitionSpec as P

MESH = pl.DeviceIdType.MESH
HIGHEST = lax.Precision.HIGHEST
COLS = 512
LANES = 128
SLAB = 80
HALF = SLAB // 2
GROUP = 8
RING = 8
CORES = 2
COL_LANE = 127
SUM_LANE = 100


def nt(a, b, precision=None):
    return lax.dot_general(
        a, b, (((1,), (1,)), ((), ())), precision=precision, preferred_element_type=jnp.float32
    )


def nn(a, b, precision=None):
    return lax.dot_general(
        a, b, (((1,), (0,)), ((), ())), precision=precision, preferred_element_type=jnp.float32
    )


def split(x):
    high = x.astype(jnp.bfloat16)
    return high, (x - high.astype(jnp.float32)).astype(jnp.bfloat16)


def iota(shape, dim):
    return lax.broadcasted_iota(jnp.int32, shape, dim)


def hops(offset):
    return min(offset, RING - offset)


def far_first():
    offsets = [(z, y) for z in range(RING) for y in range(RING)]
    return sorted(offsets, key=lambda at: -hops(at[0]) - hops(at[1]))


def for_peers(me, body):
    here_z, here_y, core = me // (RING * CORES), lax.rem(me // CORES, RING), lax.rem(me, CORES)
    at_z = [lax.rem(here_z + d, RING) * (RING * CORES) for d in range(RING)]
    at_y = [lax.rem(here_y + d, RING) * CORES for d in range(RING)]
    for z, y in far_first():
        chip = at_z[z] + at_y[y]
        for d in range(CORES):
            if z or y or d:
                body(chip + lax.rem(core + d, CORES))


def kernel(
    tiles,
    bands,
    jac,
    tile_in,
    column_in,
    weight_in,
    innovation_in,
    precision_in,
    vertical_in,
    increment,
    residual,
    jraw,
    tile_row,
    column_row,
    weight_row,
    innovation,
    precision_off,
    vertical,
    jpad,
    rmat_high,
    rmat_low,
    coef_high,
    coef_low,
    picks,
    sends,
    equal,
    repeat,
    tbuf,
    ibuf,
    own_images,
    sbuf,
    rbuf,
    w_buf,
    im_buf,
    fields,
    entered,
    in_sem,
    t_send,
    t_recv,
    i_send,
    i_recv,
    s_send,
    s_recv,
):
    me = lax.axis_index("horiz")
    lev = lax.axis_index("lev")
    obs, channels = innovation.shape
    band = jac.shape[1]
    levels = vertical.shape[1]
    used = 2 * band
    f32, bf16 = jnp.float32, jnp.bfloat16

    fetches = [
        pltpu.make_async_copy(source, target, in_sem.at[at])
        for at, (source, target) in enumerate(
            (
                (innovation_in, innovation),
                (precision_in, precision_off),
                (weight_in, weight_row),
                (tile_in, tile_row),
                (column_in, column_row),
                (jac, jraw),
                (vertical_in, vertical),
            )
        )
    ]
    for fetch in fetches:
        fetch.start()
    barrier = pltpu.get_barrier_semaphore()
    for k in range(1, bands):
        peer = lax.rem(lev + k, bands)
        pl.semaphore_signal(barrier, inc=1, device_id={"lev": peer}, device_id_type=MESH)

    def greet(semaphore, peer):
        pl.semaphore_signal(semaphore, inc=1, device_id={"horiz": peer}, device_id_type=MESH)

    plane = RING * CORES
    line_peers = [lax.rem(me + k * plane, tiles) for k in range(1, RING)]
    plane_peers = [me // plane * plane + lax.rem(me + k, plane) for k in range(1, plane)]
    for peer in line_peers + plane_peers:
        greet(barrier, peer)

    def column(row):
        return jnp.broadcast_to(row[...].astype(f32), (obs, obs)).T[:, 0:1]

    for fetch in fetches[:5]:
        fetch.wait()
    weight = column(weight_row)
    off = precision_off[...]
    eye_c = (iota((channels, channels), 0) == iota((channels, channels), 1)).astype(f32)
    rmat = eye_c + 0.5 * (off + off.T)
    rmat_high[...], rmat_low[...] = split(rmat)

    w0 = (weight * nn(innovation[...], rmat, HIGHEST)).astype(bf16)
    w_buf[0] = w0.astype(f32)

    def fill(g):
        for o in range(g * GROUP, (g + 1) * GROUP):
            start = o * SLAB
            jpad[start + 64 : start + SLAB, :] = jnp.zeros((SLAB - 64, channels), bf16)
            jpad[start : start + used, :] = jraw[o].reshape(used, channels)

    def adjoint(high, low, part, parts, total, ready=lambda g: None):
        groups = obs // GROUP // parts
        rows = groups * GROUP
        before = [jnp.zeros((rows, channels), bf16)] * part
        after = [jnp.zeros((rows, channels), bf16)] * (parts - 1 - part)
        both = jnp.concatenate([*before, high, *after, *before, low, *after], axis=0)
        lane = lax.rem(iota((SLAB, 2 * obs), 1), obs)
        for g in range(part * groups, (part + 1) * groups):
            ready(g)
            product = nt(jpad[g * GROUP * SLAB : (g + 1) * GROUP * SLAB, :], both)
            for j in range(GROUP):
                mine = lane == g * GROUP + j
                total = total + jnp.where(mine, product[j * SLAB : (j + 1) * SLAB, :], 0.0)
        return total

    def store_terms(use, t):
        t = t + pltpu.roll(t, obs, 1)
        tbuf[use, lev] = jnp.where(iota((HALF, 2 * obs), 1) < obs, t[0:HALF, :], t[HALF:, :])

    no_terms = jnp.zeros((SLAB, 2 * obs), f32)
    fetches[5].wait()
    store_terms(0, adjoint(w0, jnp.zeros_like(w0), 0, 1, no_terms, fill))

    def band_copies(buf, use, send_sem, recv_sem, part, rows):
        copies = []
        for k in range(1, bands):
            copy = pltpu.make_async_remote_copy(
                src_ref=buf.at[use, lev, rows],
                dst_ref=buf.at[use, lev, rows],
                send_sem=send_sem.at[use, part, k],
                recv_sem=recv_sem.at[use, part, k],
                device_id={"lev": lax.rem(lev + k, bands)},
                device_id_type=MESH,
            )
            copy.start()
            copies.append(copy)
        return copies

    def gather_bands(use):
        return band_copies(tbuf, use, t_send, t_recv, 0, pl.ds(0, HALF))

    pl.semaphore_wait(barrier, bands - 1 + len(line_peers) + len(plane_peers))
    copies = gather_bands(0)
    for peer in plane_peers:
        greet(entered, peer)

    onehot = (column(tile_row) == iota((obs, tiles), 1).astype(f32)).astype(f32)
    same = nt(onehot.astype(bf16), onehot.astype(bf16))
    earlier = iota((obs, obs), 1) < iota((obs, obs), 0)
    position = jnp.sum(jnp.where(earlier, same, 0.0), axis=1, keepdims=True)
    first = jnp.where(position < 0.5, onehot, 0.0)
    second = jnp.where(position > 0.5, onehot, 0.0)
    picks[:, 0:tiles] = first.astype(bf16)
    picks[:, tiles : 2 * tiles] = second.astype(bf16)
    nothing = jnp.zeros((obs, tiles), f32)
    sends[0:tiles, :] = jnp.concatenate([first, nothing], axis=0).T.astype(bf16)
    sends[tiles : 2 * tiles, :] = jnp.concatenate([second, nothing], axis=0).T.astype(bf16)
    repeat[...] = (
        iota((LANES, GROUP * SLAB), 0) == lax.rem(iota((LANES, GROUP * SLAB), 1), SLAB)
    ).astype(bf16)

    fetches[6].wait()

    row = iota((LANES, levels), 0)
    wide = iota((levels, 2 * bands * HALF), 1)
    places = lax.rem(wide, HALF) + (wide // (bands * HALF)) * HALF
    wide_level = lax.rem(wide // HALF, bands) * band + places // 2
    inside = (places < used) & (wide_level == iota(wide.shape, 0))
    eye_l = (iota((levels, levels), 0) == iota((levels, levels), 1)).astype(f32)
    both, back = 0.0, 0.0
    for v in range(2):
        factor = eye_l + vertical[v]
        own = (iota(row.shape, 1) == lev * band + row // 2) & (row < used) & (lax.rem(row, 2) == v)
        spread = jnp.where(inside & (lax.rem(places, 2) == v), 1.0, 0.0)
        own = own.astype(f32)
        both = both + nn(nt(nn(own, factor, HIGHEST), factor, HIGHEST), spread, HIGHEST)
        back = back + nn(nt(own, factor, HIGHEST), spread, HIGHEST)
    coef_high[0:LANES, :], coef_low[0:LANES, :] = split(both)
    coef_high[LANES:, :], coef_low[LANES:, :] = split(back)

    def columns(use, part):
        gathered = tbuf[use].reshape(bands * HALF, 2 * obs)
        gathered = jnp.concatenate([gathered, pltpu.roll(gathered, obs, 1)], axis=0)
        high, low = split(gathered)
        rows = pl.ds(part * LANES, LANES)
        mapped = nn(coef_high[rows, :], high) + (
            nn(coef_high[rows, :], low) + nn(coef_low[rows, :], high)
        )
        mapped = jnp.where(iota((LANES, 2 * obs), 1) < obs, mapped, 0.0)
        high, low = split(mapped)
        slots = nt(sends[...], jnp.concatenate([high, low], axis=0))
        return slots[:, 0:LANES] + slots[:, LANES:]

    def exchange(use):
        def send(peer):
            pltpu.make_async_remote_copy(
                src_ref=sbuf.at[use, peer],
                dst_ref=rbuf.at[use, me],
                send_sem=s_send.at[use],
                recv_sem=s_recv.at[use],
                device_id={"horiz": peer},
                device_id_type=MESH,
            ).start()

        for_peers(me, send)
        rbuf[use, me] = sbuf[use, me]

    def arrived(use):
        part = rbuf.at[use, pl.ds(0, tiles - 1)]
        pltpu.make_async_copy(part, part, s_recv.at[use]).wait()

    def left(use):
        part = sbuf.at[use, pl.ds(0, tiles - 1)]
        pltpu.make_async_copy(part, part, s_send.at[use]).wait()

    def put(use, slots):
        sbuf[use, :, 0, :] = slots[0:tiles, :]
        sbuf[use, :, 1, :] = slots[tiles : 2 * tiles, :]

    def got(use):
        return jnp.concatenate([rbuf[use, :, 0, :], rbuf[use, :, 1, :]], axis=0)

    def sum_at_tiles(use, first_time):
        slots = got(use)
        if first_time:
            ids = [slots[s * tiles : (s + 1) * tiles, COL_LANE : COL_LANE + 1] for s in range(2)]
            wide = [jnp.broadcast_to(one, (tiles, tiles)) for one in ids]
            tall = [one.T for one in wide]
            for a in range(2):
                for b in range(2):
                    equal[a * tiles : (a + 1) * tiles, b * tiles : (b + 1) * tiles] = jnp.where(
                        (wide[a] == tall[b]) & (wide[a] > 0.5), 1.0, 0.0
                    ).astype(bf16)
        high, low = split(slots)
        sums = nn(equal[...], jnp.concatenate([high, low], axis=1))
        put(use + 1, sums[:, 0:LANES] + sums[:, LANES:])
        return slots

    parts = 2

    def start_images(use, from_use):
        high, low = split(got(from_use))
        chosen = nn(picks[...], jnp.concatenate([high, low], axis=1)).astype(bf16)
        chosen = jnp.concatenate([chosen[:, 0:LANES], chosen[:, LANES:]], axis=0)
        spread = nn(chosen, repeat[...])
        shape = (2 * obs, GROUP * SLAB)
        spread = jnp.where(lax.rem(iota(shape, 0), GROUP) == iota(shape, 1) // SLAB, spread, 0.0)
        copies = []
        groups = obs // GROUP // parts
        for g in range(obs // GROUP):
            at = g * GROUP
            lhs = jnp.concatenate(
                [spread[at : at + GROUP, :], spread[obs + at : obs + at + GROUP, :]], axis=0
            )
            part = nn(lhs.astype(bf16), jpad[at * SLAB : (at + GROUP) * SLAB, :])
            own_images[at : at + GROUP, :] = part[0:GROUP, :] + part[GROUP:, :]
            if (g + 1) % groups == 0:
                p = g // groups
                rows = pl.ds(p * groups * GROUP, groups * GROUP)
                ibuf[use, lev, rows, :] = own_images[rows, :].astype(bf16)
                copies.append(band_copies(ibuf, use, i_send, i_recv, p, rows))
        return copies

    def weigh_images(use, copies):
        terms = no_terms
        size = obs // parts
        for p in range(parts):
            wait_all(copies[p])
            rows = slice(p * size, (p + 1) * size)
            total = own_images[rows, :]
            for k in range(1, bands):
                total = total + ibuf[use, lax.rem(lev + k, bands), rows, :].astype(f32)
            im_buf[use, rows, :] = total
            high, low = split(total)
            both = nn(jnp.concatenate([high, low], axis=0), rmat_high[...])
            w = both[0:size, :] + (both[size:, :] + nn(high, rmat_low[...]))
            w = weight[rows, :] * w
            w_buf[use + 1, rows, :] = w
            high, low = split(w)
            terms = adjoint(high, low, p, parts, terms)
        store_terms(use + 1, terms)

    def wait_all(copies):
        for copy in copies:
            copy.wait()

    column_rhs = jnp.concatenate([column(column_row) + 1.0, jnp.zeros((obs, 1), f32)], axis=0)
    column_rhs = jnp.where(iota((2 * obs, LANES), 1) == COL_LANE, column_rhs, 0.0)
    high, low = split(column_rhs)
    column_slots = nn(sends[...], high) + nn(sends[...], low)
    wait_all(copies)
    put(0, columns(0, 0) + column_slots)
    pl.semaphore_wait(entered, len(plane_peers))
    exchange(0)
    put(4, columns(0, 1))
    arrived(0)
    first_slots = sum_at_tiles(0, True)
    exchange(1)
    slot_column = first_slots[:, COL_LANE : COL_LANE + 1]
    arrived(1)
    copies = start_images(0, 1)
    exchange(4)
    weigh_images(0, copies)
    wait_all(gather_bands(1))
    put(2, columns(1, 0))
    exchange(2)
    put(5, columns(1, 1))
    arrived(2)
    sum_at_tiles(2, False)
    exchange(3)
    arrived(3)
    copies = start_images(1, 3)
    exchange(5)
    weigh_images(1, copies)
    copies = gather_bands(2)

    w0, w1, w2 = w_buf[0], w_buf[1], w_buf[2]
    im0, im1 = im_buf[0], im_buf[1]
    lane = iota((1, LANES), 1)
    scalars = jnp.zeros((1, LANES), f32)
    for at, (a, b) in enumerate(((w0, im0), (w1, im0), (w1, im1), (w2, im0), (w2, im1))):
        one = jnp.sum(jnp.sum(a * b, axis=1, keepdims=True), axis=0, keepdims=True)
        scalars = scalars + jnp.where(lane == SUM_LANE + at, one, 0.0)
    wait_all(copies)
    put(6, columns(2, 1) + scalars)
    exchange(6)

    place = (slot_column - 1.0 == iota((2 * tiles, COLS), 1).astype(f32)).astype(bf16)

    def field(slots):
        turned = jnp.concatenate([slots[0:tiles, :].T, slots[tiles:, :].T], axis=1)
        high, low = split(turned[0:SLAB, :])
        out = nn(jnp.concatenate([high, low], axis=0), place)
        return out[0:used, :] + out[SLAB : SLAB + used, :]

    arrived(4)
    fields[0] = field(got(4))
    arrived(5)
    fields[1] = field(got(5))
    arrived(6)
    last = got(6)
    sums = jnp.sum(last[0:tiles, :], axis=0, keepdims=True)
    g00, g01, g11, g02, g12 = (
        jnp.sum(jnp.where(lane == SUM_LANE + at, sums, 0.0), axis=1, keepdims=True)
        for at in range(5)
    )
    a0 = g00 / (g00 + g01)
    keep = 1.0 - a0
    rr1 = keep * keep * g00 - 2.0 * a0 * keep * g01 + a0 * a0 * g11
    k0 = keep + rr1 / g00
    k1 = -a0
    mixed = k0 + k1
    curvature = k0 * k0 * g00 + k0 * (mixed + k1) * g01 + k0 * k1 * g02 + k1 * mixed * g11
    a1 = rr1 / (curvature + k1 * k1 * g12)
    v0, v1, v2 = fields[0], fields[1], field(last)
    shape = increment.shape
    increment[...] = ((a0 + a1 * k0) * v0 + a1 * k1 * v1).reshape(shape)
    residual[...] = (
        (keep - a1 * k0) * v0 - (a0 + a1 * mixed) * v1 - a1 * k1 * v2
    ).reshape(shape)
    for use in range(7):
        left(use)


def hand_on(a_in, b_in, a_out, b_out):
    a_out[...] = a_in[...]
    b_out[...] = b_in[...]


def shards(
    tiles,
    bands,
    jacobian,
    obs_tile,
    obs_column,
    obs_weight,
    innovation,
    precision_off,
    vertical_factor,
):
    obs, variables, band, channels = jacobian.shape
    f32, bf16 = jnp.float32, jnp.bfloat16
    vmem = pl.BlockSpec(memory_space=pltpu.VMEM)
    out = jax.ShapeDtypeStruct((band, variables, COLS), f32)
    dma = pltpu.SemaphoreType.DMA
    by_level = jnp.transpose(jacobian, (0, 2, 1, 3))
    increment, residual = pl.pallas_call(
        functools.partial(kernel, tiles, bands),
        out_shape=(out, out),
        in_specs=[pl.BlockSpec(memory_space=pl.ANY)] * 7,
        out_specs=(vmem, vmem),
        scratch_shapes=[
            pltpu.VMEM(by_level.shape, bf16),
            pltpu.VMEM((1, obs), jnp.int32),
            pltpu.VMEM((1, obs), jnp.int32),
            pltpu.VMEM((1, obs), f32),
            pltpu.VMEM((obs, channels), f32),
            pltpu.VMEM((channels, channels), f32),
            pltpu.VMEM(vertical_factor.shape, f32),
            pltpu.VMEM((obs * SLAB, channels), bf16),
            pltpu.VMEM((channels, channels), bf16),
            pltpu.VMEM((channels, channels), bf16),
            pltpu.VMEM((2 * LANES, 2 * bands * HALF), bf16),
            pltpu.VMEM((2 * LANES, 2 * bands * HALF), bf16),
            pltpu.VMEM((obs, 2 * tiles), bf16),
            pltpu.VMEM((2 * tiles, 2 * obs), bf16),
            pltpu.VMEM((2 * tiles, 2 * tiles), bf16),
            pltpu.VMEM((LANES, GROUP * SLAB), bf16),
            pltpu.VMEM((3, bands, HALF, 2 * obs), f32),
            pltpu.VMEM((2, bands, obs, channels), bf16),
            pltpu.VMEM((obs, channels), f32),
            pltpu.VMEM((7, tiles, 2, LANES), f32),
            pltpu.VMEM((7, tiles, 2, LANES), f32),
            pltpu.VMEM((3, obs, channels), f32),
            pltpu.VMEM((2, obs, channels), f32),
            pltpu.VMEM((2, variables * band, COLS), f32),
            pltpu.SemaphoreType.REGULAR,
            dma((7,)),
            dma((3, 1, bands)),
            dma((3, 1, bands)),
            dma((2, 2, bands)),
            dma((2, 2, bands)),
            dma((7,)),
            dma((7,)),
        ],
        compiler_params=pltpu.CompilerParams(
            collective_id=0, has_side_effects=True, vmem_limit_bytes=60 << 20
        ),
        name="analysis",
    )(
        by_level,
        obs_tile.reshape(1, obs),
        obs_column.reshape(1, obs),
        obs_weight.reshape(1, obs),
        innovation,
        precision_off,
        vertical_factor,
    )
    return pl.pallas_call(
        hand_on,
        out_shape=(out, out),
        in_specs=[vmem] * 2,
        out_specs=[vmem] * 2,
        compiler_params=pltpu.CompilerParams(vmem_limit_bytes=60 << 20),
        name="outputs",
    )(increment, residual)


def solution(mesh):
    return jax.shard_map(
        functools.partial(shards, mesh.shape["horiz"], mesh.shape["lev"]),
        mesh=mesh,
        in_specs=(
            P("horiz", None, "lev", None),
            P("horiz", None),
            P("horiz"),
            P("horiz"),
            P("horiz", None),
            P(),
            P(),
        ),
        out_specs=(P("lev", None, "horiz"), P("lev", None, "horiz")),
        check_vma=False,
    )
```

```python
import functools

import jax
import jax.numpy as jnp
from jax import lax
from jax.experimental import pallas as pl
from jax.experimental.pallas import tpu as pltpu
from jax.sharding import PartitionSpec as P

MESH = pl.DeviceIdType.MESH
HIGHEST = lax.Precision.HIGHEST
COLS = 512
LANES = 128
SLAB = 80
HALF = SLAB // 2
GROUP = 8
CHUNKS = 2
RING = 8
CORES = 2
COL_LANE = 127
SUM_LANE = 100


def nt(a, b, precision=None):
    return lax.dot_general(
        a, b, (((1,), (1,)), ((), ())), precision=precision, preferred_element_type=jnp.float32
    )


def nn(a, b, precision=None):
    return lax.dot_general(
        a, b, (((1,), (0,)), ((), ())), precision=precision, preferred_element_type=jnp.float32
    )


def split(x):
    high = x.astype(jnp.bfloat16)
    return high, (x - high.astype(jnp.float32)).astype(jnp.bfloat16)


def iota(shape, dim):
    return lax.broadcasted_iota(jnp.int32, shape, dim)


def hops(offset):
    return min(offset, RING - offset)


def far_first():
    offsets = [(z, y) for z in range(RING) for y in range(RING)]
    return sorted(offsets, key=lambda at: -hops(at[0]) - hops(at[1]))


def for_peers(me, body):
    here_z, here_y, core = me // (RING * CORES), lax.rem(me // CORES, RING), lax.rem(me, CORES)
    at_z = [lax.rem(here_z + d, RING) * (RING * CORES) for d in range(RING)]
    at_y = [lax.rem(here_y + d, RING) * CORES for d in range(RING)]
    for z, y in far_first():
        chip = at_z[z] + at_y[y]
        for d in range(CORES):
            if z or y or d:
                body(chip + lax.rem(core + d, CORES))


def kernel(
    tiles,
    bands,
    jac,
    tile_in,
    column_in,
    weight_in,
    innovation_in,
    precision_in,
    vertical_in,
    increment,
    residual,
    jraw,
    tile_row,
    column_row,
    weight_row,
    innovation,
    precision_off,
    vertical,
    jpad,
    rmat_high,
    rmat_low,
    coef_high,
    coef_low,
    picks,
    sends,
    equal,
    repeat,
    tbuf,
    ibuf,
    own_images,
    sbuf,
    rbuf,
    w_buf,
    im_buf,
    fields,
    entered,
    in_sem,
    t_send,
    t_recv,
    i_send,
    i_recv,
    s_send,
    s_recv,
):
    me = lax.axis_index("horiz")
    lev = lax.axis_index("lev")
    obs, channels = innovation.shape
    band = jac.shape[1]
    levels = vertical.shape[1]
    used = 2 * band
    f32, bf16 = jnp.float32, jnp.bfloat16

    chunk = obs // CHUNKS
    chunks = [pl.ds(c * chunk, chunk) for c in range(CHUNKS)]
    fetches = [
        pltpu.make_async_copy(source, target, in_sem.at[at])
        for at, (source, target) in enumerate(
            (
                (innovation_in, innovation),
                (precision_in, precision_off),
                (weight_in, weight_row),
                (tile_in, tile_row),
                (column_in, column_row),
                *((jac.at[rows], jraw.at[rows]) for rows in chunks),
                (vertical_in, vertical),
            )
        )
    ]
    for fetch in fetches:
        fetch.start()
    barrier = pltpu.get_barrier_semaphore()
    for k in range(1, bands):
        peer = lax.rem(lev + k, bands)
        pl.semaphore_signal(barrier, inc=1, device_id={"lev": peer}, device_id_type=MESH)

    def greet(semaphore, peer):
        pl.semaphore_signal(semaphore, inc=1, device_id={"horiz": peer}, device_id_type=MESH)

    plane = RING * CORES
    line_peers = [lax.rem(me + k * plane, tiles) for k in range(1, RING)]
    plane_peers = [me // plane * plane + lax.rem(me + k, plane) for k in range(1, plane)]
    for peer in line_peers + plane_peers:
        greet(barrier, peer)

    def column(row):
        return jnp.broadcast_to(row[...].astype(f32), (obs, obs)).T[:, 0:1]

    for fetch in fetches[:5]:
        fetch.wait()
    weight = column(weight_row)
    off = precision_off[...]
    eye_c = (iota((channels, channels), 0) == iota((channels, channels), 1)).astype(f32)
    rmat = eye_c + 0.5 * (off + off.T)
    rmat_high[...], rmat_low[...] = split(rmat)

    w0 = (weight * nn(innovation[...], rmat, HIGHEST)).astype(bf16)
    w_buf[0] = w0.astype(f32)

    def fill(g):
        if g * GROUP % chunk == 0:
            fetches[5 + g * GROUP // chunk].wait()
        for o in range(g * GROUP, (g + 1) * GROUP):
            start = o * SLAB
            jpad[start + 64 : start + SLAB, :] = jnp.zeros((SLAB - 64, channels), bf16)
            jpad[start : start + used, :] = jraw[o].reshape(used, channels)

    def adjoint(high, low, part, parts, total, ready=lambda g: None):
        groups = obs // GROUP // parts
        rows = groups * GROUP
        before = [jnp.zeros((rows, channels), bf16)] * part
        after = [jnp.zeros((rows, channels), bf16)] * (parts - 1 - part)
        both = jnp.concatenate([*before, high, *after, *before, low, *after], axis=0)
        lane = lax.rem(iota((SLAB, 2 * obs), 1), obs)
        for g in range(part * groups, (part + 1) * groups):
            ready(g)
            product = nt(jpad[g * GROUP * SLAB : (g + 1) * GROUP * SLAB, :], both)
            for j in range(GROUP):
                mine = lane == g * GROUP + j
                total = total + jnp.where(mine, product[j * SLAB : (j + 1) * SLAB, :], 0.0)
        return total

    def store_terms(use, t):
        t = t + pltpu.roll(t, obs, 1)
        tbuf[use, lev] = jnp.where(iota((HALF, 2 * obs), 1) < obs, t[0:HALF, :], t[HALF:, :])

    no_terms = jnp.zeros((SLAB, 2 * obs), f32)
    store_terms(0, adjoint(w0, jnp.zeros_like(w0), 0, 1, no_terms, fill))

    under_way = []

    def band_copies(buf, use, send_sem, recv_sem, part, rows):
        copies = []
        for k in range(1, bands):
            copy = pltpu.make_async_remote_copy(
                src_ref=buf.at[use, lev, rows],
                dst_ref=buf.at[use, lev, rows],
                send_sem=send_sem.at[use, part, k],
                recv_sem=recv_sem.at[use, part, k],
                device_id={"lev": lax.rem(lev + k, bands)},
                device_id_type=MESH,
            )
            copy.start()
            copies.append(copy)
        under_way.extend(copies)
        return copies

    def gather_bands(use):
        return band_copies(tbuf, use, t_send, t_recv, 0, pl.ds(0, HALF))

    pl.semaphore_wait(barrier, bands - 1 + len(line_peers) + len(plane_peers))
    copies = gather_bands(0)
    for peer in plane_peers:
        greet(entered, peer)

    onehot = (column(tile_row) == iota((obs, tiles), 1).astype(f32)).astype(f32)
    same = nt(onehot.astype(bf16), onehot.astype(bf16))
    earlier = iota((obs, obs), 1) < iota((obs, obs), 0)
    position = jnp.sum(jnp.where(earlier, same, 0.0), axis=1, keepdims=True)
    first = jnp.where(position < 0.5, onehot, 0.0)
    second = jnp.where(position > 0.5, onehot, 0.0)
    picks[:, 0:tiles] = first.astype(bf16)
    picks[:, tiles : 2 * tiles] = second.astype(bf16)
    nothing = jnp.zeros((obs, tiles), f32)
    sends[0:tiles, :] = jnp.concatenate([first, nothing], axis=0).T.astype(bf16)
    sends[tiles : 2 * tiles, :] = jnp.concatenate([second, nothing], axis=0).T.astype(bf16)
    repeat[...] = (
        iota((LANES, GROUP * SLAB), 0) == lax.rem(iota((LANES, GROUP * SLAB), 1), SLAB)
    ).astype(bf16)

    fetches[-1].wait()

    row = iota((LANES, levels), 0)
    wide = iota((levels, 2 * bands * HALF), 1)
    places = lax.rem(wide, HALF) + (wide // (bands * HALF)) * HALF
    wide_level = lax.rem(wide // HALF, bands) * band + places // 2
    inside = (places < used) & (wide_level == iota(wide.shape, 0))
    eye_l = (iota((levels, levels), 0) == iota((levels, levels), 1)).astype(f32)
    both, back = 0.0, 0.0
    for v in range(2):
        factor = eye_l + vertical[v]
        own = (iota(row.shape, 1) == lev * band + row // 2) & (row < used) & (lax.rem(row, 2) == v)
        spread = jnp.where(inside & (lax.rem(places, 2) == v), 1.0, 0.0)
        own = own.astype(f32)
        both = both + nn(nt(nn(own, factor, HIGHEST), factor, HIGHEST), spread, HIGHEST)
        back = back + nn(nt(own, factor, HIGHEST), spread, HIGHEST)
    coef_high[0:LANES, :], coef_low[0:LANES, :] = split(both)
    coef_high[LANES:, :], coef_low[LANES:, :] = split(back)

    def columns(use, part):
        gathered = tbuf[use].reshape(bands * HALF, 2 * obs)
        gathered = jnp.concatenate([gathered, pltpu.roll(gathered, obs, 1)], axis=0)
        high, low = split(gathered)
        rows = pl.ds(part * LANES, LANES)
        mapped = nn(coef_high[rows, :], jnp.concatenate([high, low], axis=1))
        mapped = mapped[:, 0 : 2 * obs] + (mapped[:, 2 * obs :] + nn(coef_low[rows, :], high))
        mapped = jnp.where(iota((LANES, 2 * obs), 1) < obs, mapped, 0.0)
        high, low = split(mapped)
        slots = nt(sends[...], jnp.concatenate([high, low], axis=0))
        return slots[:, 0:LANES] + slots[:, LANES:]

    def exchange(use):
        def send(peer):
            pltpu.make_async_remote_copy(
                src_ref=sbuf.at[use, peer],
                dst_ref=rbuf.at[use, me],
                send_sem=s_send.at[use],
                recv_sem=s_recv.at[use],
                device_id={"horiz": peer},
                device_id_type=MESH,
            ).start()

        for_peers(me, send)
        rbuf[use, me] = sbuf[use, me]

    def arrived(use):
        part = rbuf.at[use, pl.ds(0, tiles - 1)]
        pltpu.make_async_copy(part, part, s_recv.at[use]).wait()

    def left(use):
        part = sbuf.at[use, pl.ds(0, tiles - 1)]
        pltpu.make_async_copy(part, part, s_send.at[use]).wait()

    def put(use, slots):
        sbuf[use, :, 0, :] = slots[0:tiles, :]
        sbuf[use, :, 1, :] = slots[tiles : 2 * tiles, :]

    def got(use):
        return jnp.concatenate([rbuf[use, :, 0, :], rbuf[use, :, 1, :]], axis=0)

    def sum_at_tiles(use, first_time):
        slots = got(use)
        if first_time:
            ids = [slots[s * tiles : (s + 1) * tiles, COL_LANE : COL_LANE + 1] for s in range(2)]
            wide = [jnp.broadcast_to(one, (tiles, tiles)) for one in ids]
            tall = [one.T for one in wide]
            for a in range(2):
                for b in range(2):
                    equal[a * tiles : (a + 1) * tiles, b * tiles : (b + 1) * tiles] = jnp.where(
                        (wide[a] == tall[b]) & (wide[a] > 0.5), 1.0, 0.0
                    ).astype(bf16)
        high, low = split(slots)
        sums = nn(equal[...], jnp.concatenate([high, low], axis=1))
        put(use + 1, sums[:, 0:LANES] + sums[:, LANES:])
        return slots

    parts = 2

    def start_images(use, from_use):
        high, low = split(got(from_use))
        chosen = nn(picks[...], jnp.concatenate([high, low], axis=1)).astype(bf16)
        chosen = jnp.concatenate([chosen[:, 0:LANES], chosen[:, LANES:]], axis=0)
        spread = nn(chosen, repeat[...])
        shape = (2 * obs, GROUP * SLAB)
        spread = jnp.where(lax.rem(iota(shape, 0), GROUP) == iota(shape, 1) // SLAB, spread, 0.0)
        copies = []
        groups = obs // GROUP // parts
        for g in range(obs // GROUP):
            at = g * GROUP
            lhs = jnp.concatenate(
                [spread[at : at + GROUP, :], spread[obs + at : obs + at + GROUP, :]], axis=0
            )
            part = nn(lhs.astype(bf16), jpad[at * SLAB : (at + GROUP) * SLAB, :])
            own_images[at : at + GROUP, :] = part[0:GROUP, :] + part[GROUP:, :]
            if (g + 1) % groups == 0:
                p = g // groups
                rows = pl.ds(p * groups * GROUP, groups * GROUP)
                ibuf[use, lev, rows, :] = own_images[rows, :].astype(bf16)
                copies.append(band_copies(ibuf, use, i_send, i_recv, p, rows))
        return copies

    def weigh_images(use, copies):
        terms = no_terms
        size = obs // parts
        for p in range(parts):
            wait_all(copies[p])
            rows = slice(p * size, (p + 1) * size)
            total = own_images[rows, :]
            for k in range(1, bands):
                total = total + ibuf[use, lax.rem(lev + k, bands), rows, :].astype(f32)
            im_buf[use, rows, :] = total
            high, low = split(total)
            both = nn(jnp.concatenate([high, low], axis=0), rmat_high[...])
            w = both[0:size, :] + (both[size:, :] + nn(high, rmat_low[...]))
            w = weight[rows, :] * w
            w_buf[use + 1, rows, :] = w
            high, low = split(w)
            terms = adjoint(high, low, p, parts, terms)
        store_terms(use + 1, terms)

    def wait_all(copies):
        for copy in copies:
            copy.wait_recv()

    column_rhs = jnp.concatenate([column(column_row) + 1.0, jnp.zeros((obs, 1), f32)], axis=0)
    column_rhs = jnp.where(iota((2 * obs, LANES), 1) == COL_LANE, column_rhs, 0.0)
    high, low = split(column_rhs)
    column_slots = nn(sends[...], high) + nn(sends[...], low)
    wait_all(copies)
    put(0, columns(0, 0) + column_slots)
    pl.semaphore_wait(entered, len(plane_peers))
    exchange(0)
    put(4, columns(0, 1))
    arrived(0)
    first_slots = sum_at_tiles(0, True)
    exchange(1)
    slot_column = first_slots[:, COL_LANE : COL_LANE + 1]
    arrived(1)
    copies = start_images(0, 1)
    exchange(4)
    weigh_images(0, copies)
    wait_all(gather_bands(1))
    put(2, columns(1, 0))
    exchange(2)
    put(5, columns(1, 1))
    arrived(2)
    sum_at_tiles(2, False)
    exchange(3)
    arrived(3)
    copies = start_images(1, 3)
    exchange(5)
    weigh_images(1, copies)
    copies = gather_bands(2)

    w0, w1, w2 = w_buf[0], w_buf[1], w_buf[2]
    im0, im1 = im_buf[0], im_buf[1]
    lane = iota((1, LANES), 1)
    scalars = jnp.zeros((1, LANES), f32)
    for at, (a, b) in enumerate(((w0, im0), (w1, im0), (w1, im1), (w2, im0), (w2, im1))):
        one = jnp.sum(jnp.sum(a * b, axis=1, keepdims=True), axis=0, keepdims=True)
        scalars = scalars + jnp.where(lane == SUM_LANE + at, one, 0.0)
    wait_all(copies)
    put(6, columns(2, 1) + scalars)
    exchange(6)

    place = (slot_column - 1.0 == iota((2 * tiles, COLS), 1).astype(f32)).astype(bf16)

    def field(slots):
        turned = jnp.concatenate([slots[0:tiles, :].T, slots[tiles:, :].T], axis=1)
        high, low = split(turned[0:SLAB, :])
        out = nn(jnp.concatenate([high, low], axis=0), place)
        return out[0:used, :] + out[SLAB : SLAB + used, :]

    arrived(4)
    fields[0] = field(got(4))
    arrived(5)
    fields[1] = field(got(5))
    arrived(6)
    last = got(6)
    sums = jnp.sum(last[0:tiles, :], axis=0, keepdims=True)
    g00, g01, g11, g02, g12 = (
        jnp.sum(jnp.where(lane == SUM_LANE + at, sums, 0.0), axis=1, keepdims=True)
        for at in range(5)
    )
    a0 = g00 / (g00 + g01)
    keep = 1.0 - a0
    rr1 = keep * keep * g00 - 2.0 * a0 * keep * g01 + a0 * a0 * g11
    k0 = keep + rr1 / g00
    k1 = -a0
    mixed = k0 + k1
    curvature = k0 * k0 * g00 + k0 * (mixed + k1) * g01 + k0 * k1 * g02 + k1 * mixed * g11
    a1 = rr1 / (curvature + k1 * k1 * g12)
    v0, v1, v2 = fields[0], fields[1], field(last)
    shape = increment.shape
    increment[...] = ((a0 + a1 * k0) * v0 + a1 * k1 * v1).reshape(shape)
    residual[...] = (
        (keep - a1 * k0) * v0 - (a0 + a1 * mixed) * v1 - a1 * k1 * v2
    ).reshape(shape)
    for copy in under_way:
        copy.wait_send()
    for use in range(7):
        left(use)


def hand_on(a_in, b_in, a_out, b_out):
    a_out[...] = a_in[...]
    b_out[...] = b_in[...]


def shards(
    tiles,
    bands,
    jacobian,
    obs_tile,
    obs_column,
    obs_weight,
    innovation,
    precision_off,
    vertical_factor,
):
    obs, variables, band, channels = jacobian.shape
    f32, bf16 = jnp.float32, jnp.bfloat16
    vmem = pl.BlockSpec(memory_space=pltpu.VMEM)
    out = jax.ShapeDtypeStruct((band, variables, COLS), f32)
    dma = pltpu.SemaphoreType.DMA
    by_level = jnp.transpose(jacobian, (0, 2, 1, 3))
    increment, residual = pl.pallas_call(
        functools.partial(kernel, tiles, bands),
        out_shape=(out, out),
        in_specs=[pl.BlockSpec(memory_space=pl.ANY)] * 7,
        out_specs=(vmem, vmem),
        scratch_shapes=[
            pltpu.VMEM(by_level.shape, bf16),
            pltpu.VMEM((1, obs), jnp.int32),
            pltpu.VMEM((1, obs), jnp.int32),
            pltpu.VMEM((1, obs), f32),
            pltpu.VMEM((obs, channels), f32),
            pltpu.VMEM((channels, channels), f32),
            pltpu.VMEM(vertical_factor.shape, f32),
            pltpu.VMEM((obs * SLAB, channels), bf16),
            pltpu.VMEM((channels, channels), bf16),
            pltpu.VMEM((channels, channels), bf16),
            pltpu.VMEM((2 * LANES, 2 * bands * HALF), bf16),
            pltpu.VMEM((2 * LANES, 2 * bands * HALF), bf16),
            pltpu.VMEM((obs, 2 * tiles), bf16),
            pltpu.VMEM((2 * tiles, 2 * obs), bf16),
            pltpu.VMEM((2 * tiles, 2 * tiles), bf16),
            pltpu.VMEM((LANES, GROUP * SLAB), bf16),
            pltpu.VMEM((3, bands, HALF, 2 * obs), f32),
            pltpu.VMEM((2, bands, obs, channels), bf16),
            pltpu.VMEM((obs, channels), f32),
            pltpu.VMEM((7, tiles, 2, LANES), f32),
            pltpu.VMEM((7, tiles, 2, LANES), f32),
            pltpu.VMEM((3, obs, channels), f32),
            pltpu.VMEM((2, obs, channels), f32),
            pltpu.VMEM((2, variables * band, COLS), f32),
            pltpu.SemaphoreType.REGULAR,
            dma((6 + CHUNKS,)),
            dma((3, 1, bands)),
            dma((3, 1, bands)),
            dma((2, 2, bands)),
            dma((2, 2, bands)),
            dma((7,)),
            dma((7,)),
        ],
        compiler_params=pltpu.CompilerParams(
            collective_id=0, has_side_effects=True, vmem_limit_bytes=60 << 20
        ),
        name="analysis",
    )(
        by_level,
        obs_tile.reshape(1, obs),
        obs_column.reshape(1, obs),
        obs_weight.reshape(1, obs),
        innovation,
        precision_off,
        vertical_factor,
    )
    return pl.pallas_call(
        hand_on,
        out_shape=(out, out),
        in_specs=[vmem] * 2,
        out_specs=[vmem] * 2,
        compiler_params=pltpu.CompilerParams(vmem_limit_bytes=60 << 20),
        name="outputs",
    )(increment, residual)


def solution(mesh):
    return jax.shard_map(
        functools.partial(shards, mesh.shape["horiz"], mesh.shape["lev"]),
        mesh=mesh,
        in_specs=(
            P("horiz", None, "lev", None),
            P("horiz", None),
            P("horiz"),
            P("horiz"),
            P("horiz", None),
            P(),
            P(),
        ),
        out_specs=(P("lev", None, "horiz"), P("lev", None, "horiz")),
        check_vma=False,
    )
```
